256 devices in a mesh: row: 32 (over x_lo, z, core), col: 8 (over y, x_hi).
Axes of the slice: x: 4 (x_hi: 2, x_lo: 2; x = x_hi * 2 + x_lo), y: 4, z: 8, core: 2. Of those that a mesh axis runs over, the one named last changes fastest.
Arguments:
- tokens: bfloat16 [512, 12288], P('row', 'col'), may hold values from -6 to 6
- cotangent: bfloat16 [512, 12288], P('row', 'col'), may hold values from -40 to 40
- up_weight: bfloat16 [12288, 24576], P('col', 'row'), may hold values from -0.078125 to 0.078125
- down_weight: bfloat16 [24576, 12288], P('row', 'col'), may hold values from -0.0546875 to 0.0546875
- up_keep: int32 [96, 192], P('col', 'row'), may hold values 0 or 1
- down_keep: int32 [192, 96], P('row', 'col'), may hold values 0 or 1
- clip_norms: int32 [4], replicated, may hold values from 200 to 1999
Outputs:
- output: bfloat16 [512, 12288], P('row', 'col')
- input_grad: bfloat16 [512, 12288], P('row', 'col')
- up_update: bfloat16 [12288, 24576], P('col', 'row')
- down_update: bfloat16 [24576, 12288], P('row', 'col')
The draws below stay inside these ranges and needn't reach their ends.
All inputs are finite; a program needn't handle non-finite values. No bound on the sum of `up_keep` or of `down_keep` on one device may be relied on, other than what follows from the above.
Results may differ from the reference program's by a relative error of at most 0.0056.
Values may be sent and summed in bfloat16 or wider, within the bound.
A program may use at most 64 MiB of HBM per device.

```python
import math
import jax
import jax.numpy as jnp

D = 12288
FF = 24576
BLK = 128
EX = 4
SEQ = 128
TOKENS = 512


def draw_cotangent(key, part):
    key = jax.random.fold_in(key, 5)
    scale_key, value_key = jax.random.split(key)
    scales = jnp.exp(jax.random.uniform(scale_key, (EX,), jnp.float32, math.log(0.5), math.log(5.0)))
    values = jnp.clip(jax.random.normal(value_key, (EX, SEQ, D), jnp.float32), -7.0, 7.0)
    return (values * scales[:, None, None]).reshape(TOKENS, D).astype(jnp.bfloat16)


def plant(values, stream_key, smallest, high):
    place = [jax.random.randint(jax.random.fold_in(stream_key, axis), (), 0, length) for axis, length in enumerate(values.shape)]
    widest = values.shape.index(max(values.shape))
    next_to = place[:widest] + [(place[widest] + 1) % values.shape[widest]] + place[widest + 1:]
    return values.at[tuple(place)].set(smallest).at[tuple(next_to)].set(high)


def block_levels(key, extent, shards, smallest, high):
    level, own = 1.0, jax.random.fold_in(key, 6)
    for dim, shards_of in shards:
        steps = jnp.exp(jax.random.uniform(jax.random.fold_in(own, dim), (shards_of,), jnp.float32, smallest / len(shards), high / len(shards)))
        level = level * jnp.repeat(steps, extent[dim] // shards_of).reshape([-1 if axis == dim else 1 for axis in range(len(extent))])
    return level


def gaussian(key, dims, width, limit, pieces=(), kind=jnp.bfloat16):
    drawn = jax.random.normal(key, dims, jnp.float32) * width
    if len(pieces) > 0:
        drawn = block_levels(key, dims, pieces, -0.22, 0.18) * drawn
    return jnp.clip(drawn, min=-limit, max=limit).astype(kind)


def setup_inputs(seed: int = 0) -> dict:
    streams_of = jax.random.split(jax.random.key(seed), 8)
    return {
        "tokens": gaussian(streams_of[0], (TOKENS, D), 1.0, 6.0, ((0, 32), (1, 8))),
        "cotangent": draw_cotangent(jax.random.fold_in(streams_of[7], 71), 0),
        "up_weight": gaussian(streams_of[2], (D, FF), (D // 2) ** -0.5, 0.078125, ((0, 8), (1, 32))),
        "down_weight": gaussian(streams_of[3], (FF, D), (FF // 2) ** -0.5, 0.0546875, ((0, 32), (1, 8))),
        "up_keep": plant((jax.random.randint(streams_of[4], (D // BLK, FF // BLK), 0, 2) < 1).astype(jnp.int32), jax.random.fold_in(streams_of[4], 1), 0, 1),
        "down_keep": plant((jax.random.randint(streams_of[5], (FF // BLK, D // BLK), 0, 2) < 1).astype(jnp.int32), jax.random.fold_in(streams_of[5], 1), 0, 1),
        "clip_norms": plant(jax.random.randint(streams_of[6], (EX,), 200, 2000), jax.random.fold_in(streams_of[6], 1), 200, 1999).astype(jnp.int32),
    }


def gelu_tanh(value):
    return jax.nn.gelu(value, approximate=True)

def expand(keep):
    return jnp.repeat(jnp.repeat(keep.astype(jnp.bfloat16), BLK, 0), BLK, 1)

def reference(tokens, cotangent, up_weight, down_weight, up_keep, down_keep, clip_norms):
    up_mask = expand(up_keep)
    down_mask = expand(down_keep)
    up_masked = up_weight * up_mask
    down_masked = down_weight * down_mask
    pre = jnp.dot(tokens, up_masked, preferred_element_type=jnp.float32)
    act_full, gelu_back = jax.vjp(gelu_tanh, pre)
    act = act_full.astype(jnp.bfloat16)
    output = jnp.dot(act, down_masked, preferred_element_type=jnp.float32).astype(jnp.bfloat16)
    act_grad = jnp.dot(cotangent, down_masked.T, preferred_element_type=jnp.float32)
    pre_grad = gelu_back(act_grad)[0].astype(jnp.bfloat16)
    input_grad = jnp.dot(pre_grad, up_masked.T, preferred_element_type=jnp.float32).astype(jnp.bfloat16)
    squares = []
    for example in range(EX):
        lo_row = example * SEQ
        first = jnp.dot(tokens[lo_row:lo_row + SEQ].T, pre_grad[lo_row:lo_row + SEQ], preferred_element_type=jnp.float32) * up_mask
        second = jnp.dot(act[lo_row:lo_row + SEQ].T, cotangent[lo_row:lo_row + SEQ], preferred_element_type=jnp.float32) * down_mask
        squares.append(jnp.sum(first * first) + jnp.sum(second * second))
    squared = jnp.stack(squares)
    bound = clip_norms.astype(jnp.float32) * (math.sqrt(D * FF * SEQ) / 1000.0)
    factor = jnp.minimum(jnp.float32(1.0), bound / jnp.sqrt(squared + 1e-06))
    row_factor = jnp.repeat(factor, SEQ)[:, None]
    pre_scaled = (pre_grad.astype(jnp.float32) * row_factor).astype(jnp.bfloat16)
    cot_scaled = (cotangent.astype(jnp.float32) * row_factor).astype(jnp.bfloat16)
    unit = 7.0 / (EX * math.sqrt(SEQ))
    up_update = (jnp.dot(tokens.T, pre_scaled, preferred_element_type=jnp.float32) * up_mask * unit).astype(jnp.bfloat16)
    down_update = (jnp.dot(act.T, cot_scaled, preferred_element_type=jnp.float32) * down_mask * unit).astype(jnp.bfloat16)
    return (output, input_grad, up_update, down_update)
```

```python
import functools
import math

import jax
import jax.numpy as jnp
from jax import lax
from jax.experimental import pallas as pl
from jax.experimental.pallas import tpu as pltpu
from jax.sharding import PartitionSpec as P

MESH = pl.DeviceIdType.MESH
D = 12288
FF = 24576
SEQ = 128
BLK = 128
EX = 4
SUB = 16
F32 = jnp.float32
BF16 = jnp.bfloat16
ROOT = math.sqrt(2.0 / math.pi)
UNIT = 7.0 / (EX * math.sqrt(SEQ))
BOUND = math.sqrt(D * FF * SEQ) / 1000.0


def dot(a, b, ca, cb):
    return lax.dot_general(a, b, (((ca,), (cb,)), ((), ())), preferred_element_type=F32)


def kernel(
    nz, nc,
    tok, cot, up, dn, upk, dnk, clip,
    out_o, ing_o, up_o, dn_o,
    tokp, cotp, upm, dnm, mu, md,
    send_h, recv_h, hid, pg, dact,
    part, pair, pair_r, ring_s, ring_r, fin, fin_s, fin_r,
    sq_a, sq_s, sq_r, psc, csc, uo, do,
    loc_sem, ag_s, ag_r, col_s, col_r, row_s, row_r, sq_ss, sq_rs,
):
    tokens = tok.shape[0] * 4 * nz
    width = tok.shape[1]
    hidden = up.shape[1]
    r = lax.axis_index("row")
    c = lax.axis_index("col")
    core = lax.rem(r, 2)
    z = lax.rem(lax.div(r, 2), nz)
    x = lax.div(r, 2 * nz)

    def row_of(xx, zz, kk):
        return (xx * nz + zz) * 2 + kk

    def zmod(v):
        return lax.rem(v + 2 * nz, nz)

    me = (r, c)
    core_dev = (row_of(x, z, 1 - core), c)
    x_dev = (row_of(1 - x, z, core), c)
    xc_dev = (row_of(1 - x, z, 1 - core), c)
    z_dev = [(row_of(x, zmod(z + 1), core), c), (row_of(x, zmod(z - 1), core), c)]

    def z_at(k):
        return (row_of(x, zmod(z + k), core), c)

    def c_at(k):
        return (r, lax.rem(c + k, nc))

    up_in = pltpu.make_async_copy(up, upm, loc_sem.at[0])
    dn_in = pltpu.make_async_copy(dn, dnm, loc_sem.at[1])
    up_in.start()
    dn_in.start()

    def rows(ref, xx, zz, kk):
        return ref.at[pl.ds(pl.multiple_of(row_of(xx, zz, kk) * SUB, SUB), SUB)]

    own = [
        pltpu.make_async_copy(tok, rows(tokp, x, z, core), loc_sem.at[2]),
        pltpu.make_async_copy(cot, rows(cotp, x, z, core), loc_sem.at[3]),
    ]
    own[0].start()
    own[1].start()

    barrier = pltpu.get_barrier_semaphore()
    peers = [core_dev, x_dev, xc_dev]
    peers += [z_at(k) for k in range(1, nz)]
    peers += [c_at(k) for k in range(1, nc)]
    for dev in peers:
        pl.semaphore_signal(barrier, inc=1, device_id=dev, device_id_type=MESH)
    pl.semaphore_wait(barrier, len(peers))

    pending = []

    def send(src, dst, ssem, rsem, dev):
        copy = pltpu.make_async_remote_copy(
            src_ref=src, dst_ref=dst, send_sem=ssem, recv_sem=rsem, device_id=dev, device_id_type=MESH
        )
        copy.start()
        pending.append(copy)
        return copy

    def arrived(dst, rsem, dev):
        pltpu.make_async_remote_copy(
            src_ref=dst, dst_ref=dst, send_sem=rsem, recv_sem=rsem, device_id=dev, device_id_type=MESH
        ).wait_recv()

    half = nz // 2
    reach = [[half, half - 1], [half - 1, half]]
    n_ring = 4 * half

    def ring_id(stream, way, step):
        return 1 + (stream * 2 + way) * half + step

    core_base = 1 + n_ring

    class Gather:
        def __init__(self, a, shard, panel):
            self.a, self.shard, self.panel = a, shard, panel

        def sems(self, k):
            return ag_s.at[self.a, k], ag_r.at[self.a, k]

        def slot(self, stream, off):
            xx = x if stream == 0 else 1 - x
            return rows(self.panel, xx, zmod(z + off), core)

        def to_core(self, stream, off, src=None):
            dst = self.slot(stream, off)
            k = core_base + stream * nz + (off % nz)
            send(dst if src is None else src, dst, *self.sems(k), core_dev)

        def start(self):
            dst = self.slot(0, 0)
            send(self.shard, dst, *self.sems(0), x_dev)
            for way in (0, 1):
                send(self.shard, dst, *self.sems(ring_id(0, way, 0)), z_dev[way])
            self.to_core(0, 0, self.shard)

        def start_partner(self):
            dst = self.slot(1, 0)
            arrived(dst, self.sems(0)[1], x_dev)
            for way in (0, 1):
                send(dst, dst, *self.sems(ring_id(1, way, 0)), z_dev[way])
            self.to_core(1, 0)

        def step(self, s):
            for stream in (0, 1):
                for way in (0, 1):
                    if s - 1 >= reach[stream][way]:
                        continue
                    off = -s if way == 0 else s
                    src = self.slot(stream, off)
                    arrived(src, self.sems(ring_id(stream, way, s - 1))[1], z_dev[1 - way])
                    if s < reach[stream][way]:
                        send(src, src, *self.sems(ring_id(stream, way, s)), z_dev[way])
                    self.to_core(stream, off)

        def finish(self):
            for stream in (0, 1):
                for off in range(nz):
                    xx = x if stream == 0 else 1 - x
                    dst = rows(self.panel, xx, zmod(z + off), 1 - core)
                    arrived(dst, self.sems(core_base + stream * nz + off)[1], core_dev)

    gt = Gather(0, tok, tokp)
    gc = Gather(1, cot, cotp)
    gt.start()
    gt.start_partner()
    gt.step(1)
    gt.step(2)
    gc.start()
    gc.start_partner()

    nbu, nbh = width // BLK, hidden // BLK
    for i in range(nbu):
        for j in range(nbh):
            mu[i : i + 1, j * BLK : (j + 1) * BLK] = jnp.full((1, BLK), upk[i, j].astype(F32))
            md[j : j + 1, i * BLK : (i + 1) * BLK] = jnp.full((1, BLK), dnk[j, i].astype(F32))
    up_in.wait()

    @pl.loop(0, nbu)
    def _(i):
        at = pl.ds(pl.multiple_of(i * BLK, BLK), BLK)
        upm[at, :] = upm[at, :] * mu[pl.ds(i, 1), :].astype(BF16)

    gt.step(3)
    dn_in.wait()

    @pl.loop(0, nbh)
    def _(j):
        at = pl.ds(pl.multiple_of(j * BLK, BLK), BLK)
        dnm[at, :] = dnm[at, :] * md[pl.ds(j, 1), :].astype(BF16)

    for s in range(4, half + 1):
        gt.step(s)
    own[0].wait()
    gt.finish()

    blk = tokens // nc
    chunk = 256
    per = chunk // blk
    n_chunk = tokens // chunk

    def col_send(a, src, dst, q, k):
        return send(src, dst, col_s.at[a, k], col_r.at[a, k], (r, q))

    def scatter_chunk(a, m, value):
        for b in range(per):
            send_h[a, m * per + b] = value[b * blk : (b + 1) * blk].astype(BF16)

    def scatter_send(a):
        for k in range(1, nc):
            q = lax.rem(c + k, nc)
            col_send(a, send_h.at[a, q], recv_h.at[a, k], q, k)

    def scatter_sum(a):
        total = send_h[a, c].astype(F32)
        for k in range(1, nc):
            arrived(recv_h.at[a, k], col_r.at[a, k], c_at(nc - k))
            total += recv_h[a, k].astype(F32)
        return total

    def gather_send(a, panel):
        for k in range(1, nc):
            col_send(a, panel.at[c], panel.at[c], lax.rem(c + k, nc), k)

    def gather_wait(a, panel):
        for k in range(1, nc):
            q = lax.rem(c + nc - k, nc)
            arrived(panel.at[q], col_r.at[a, k], (r, q))

    for m in range(n_chunk):
        scatter_chunk(0, m, dot(tokp[m * chunk : (m + 1) * chunk], upm[...], 1, 0))
    scatter_send(0)

    for s in range(1, half + 1):
        gc.step(s)
    own[1].wait()
    gc.finish()

    for m in range(n_chunk):
        scatter_chunk(1, m, dot(cotp[m * chunk : (m + 1) * chunk], dnm[...], 1, 1))

    v = scatter_sum(0)
    t = jnp.tanh(ROOT * (v + 0.044715 * (v * v * v)))
    hid[c] = (0.5 * v * (1.0 + t)).astype(BF16)
    gather_send(2, hid)
    dact[...] = 0.5 * (1.0 + t) + (0.5 * ROOT) * v * (1.0 - t * t) * (1.0 + 0.134145 * (v * v))
    scatter_send(1)

    g = scatter_sum(1)
    pg[c] = (g * dact[...]).astype(BF16)
    gather_send(3, pg)

    class RowSum:
        def __init__(self, a):
            self.a = a

        def sems(self, k):
            return row_s.at[self.a, k], row_r.at[self.a, k]

        def rows_of(self, m, value):
            v4 = value.reshape(nz, 2, SUB, width)
            part[0, m] = v4[:, 0]
            part[1, m] = v4[:, 1]
            pair[self.a, 0, m] = v4[:, 0].astype(BF16)
            pair[self.a, 1, m] = v4[:, 1].astype(BF16)
            send(pair.at[self.a, 1 - core, m], pair_r.at[self.a, m], *self.sems(m), core_dev)

        def pair_wait(self, m):
            arrived(pair_r.at[self.a, m], self.sems(m)[1], core_dev)

        def q(self, m, zz):
            return part[core, m, zz] + pair_r[self.a, m, zz].astype(F32)

        def step(self, s):
            a = self.a
            for way in (0, 1):
                off = half + 1 - s
                zz = zmod(z + off) if way == 0 else zmod(z - off)
                k = 2 + way * half + (s - 1)
                if s > 1:
                    pk = 2 + way * half + (s - 2)
                    if s == 2:
                        arrived(ring_r.at[a, way, 0, way], self.sems(pk)[1], z_dev[1 - way])
                    else:
                        arrived(ring_r.at[a, way, s - 2], self.sems(pk)[1], z_dev[1 - way])
                for m in (0, 1):
                    if s == 1 and m != way:
                        continue
                    val = self.q(m, zz)
                    if s > 2 or (s == 2 and m == way):
                        val += ring_r[a, way, s - 2, m].astype(F32)
                    ring_s[a, way, s - 1, m] = val.astype(BF16)
                if s == 1:
                    send(ring_s.at[a, way, 0, way], ring_r.at[a, way, 0, way], *self.sems(k), z_dev[way])
                else:
                    send(ring_s.at[a, way, s - 1], ring_r.at[a, way, s - 1], *self.sems(k), z_dev[way])

        def last(self):
            a = self.a
            for way in (0, 1):
                k = 2 + way * half + half - 1
                arrived(ring_r.at[a, way, half - 1], self.sems(k)[1], z_dev[1 - way])
            for m in (0, 1):
                val = self.q(m, z)
                val += ring_r[a, 0, half - 1, m].astype(F32)
                val += ring_r[a, 1, half - 1, m].astype(F32)
                fin[m] = val
                fin_s[a, m] = val.astype(BF16)
            send(fin_s.at[a, 1 - x], fin_r.at[a], *self.sems(2 + 2 * half), x_dev)

        def result(self, o):
            mine = fin[x]
            arrived(fin_r.at[self.a], self.sems(2 + 2 * half)[1], x_dev)
            o[...] = (mine + fin_r[self.a].astype(F32)).astype(BF16)

    def flat(ref, m):
        per_m = chunk // blk
        return ref[m * per_m : (m + 1) * per_m].reshape(chunk, hidden)

    def example(ref, e):
        n = SEQ // blk
        return ref[e * n : (e + 1) * n].reshape(SEQ, hidden)

    def norm_down(e):
        cote = cotp[e * SEQ : (e + 1) * SEQ]
        he = example(hid, e)
        acc = jnp.zeros((1, width), F32)
        for j in range(nbh):
            gg = dot(he[:, j * BLK : (j + 1) * BLK], cote, 0, 0)
            acc += jnp.sum(gg * gg, axis=0, keepdims=True) * md[j : j + 1, :]
        return jnp.sum(acc)

    def norm_up(e):
        toke = tokp[e * SEQ : (e + 1) * SEQ]
        pge = example(pg, e)
        acc = jnp.zeros((1, hidden), F32)
        for i in range(nbu):
            gg = dot(toke[:, i * BLK : (i + 1) * BLK], pge, 0, 0)
            acc += jnp.sum(gg * gg, axis=0, keepdims=True) * mu[i : i + 1, :]
        return jnp.sum(acc)

    ro = RowSum(0)
    gather_wait(2, hid)
    for m in range(2):
        ro.rows_of(m, dot(flat(hid, m), dnm[...], 1, 0))
    ro.pair_wait(0)
    ro.pair_wait(1)
    down_sq = []
    for s in range(1, half + 1):
        ro.step(s)
        if s <= EX:
            down_sq.append(norm_down(s - 1))
    ro.last()
    ro.result(out_o)

    ri = RowSum(1)
    gather_wait(3, pg)
    for m in range(2):
        ri.rows_of(m, dot(flat(pg, m), upm[...], 1, 1))
    up_sq = [norm_up(0)]
    ri.pair_wait(0)
    ri.pair_wait(1)
    ri.step(1)
    up_sq += [norm_up(1), norm_up(2)]
    ri.step(2)
    up_sq += [norm_up(3)]

    groups = [
        [(c_at(k), c_at(nc - k)) for k in range(1, nc)],
        [(z_at(k), z_at(nz - k)) for k in range(1, nz)],
        [(core_dev, core_dev), (x_dev, x_dev), (xc_dev, xc_dev)],
    ]

    def sq_send(g):
        sq_s[g] = sq_a[...]
        for k, (dev, _) in enumerate(groups[g]):
            send(sq_s.at[g], sq_r.at[g, k], sq_ss.at[g, k], sq_rs.at[g, k], dev)

    def sq_sum(g):
        total = sq_a[...]
        for k, (_, dev) in enumerate(groups[g]):
            arrived(sq_r.at[g, k], sq_rs.at[g, k], dev)
            total += sq_r[g, k]
        sq_a[...] = total

    sq_a[...] = jnp.zeros_like(sq_a)
    for e in range(EX):
        sq_a[e : e + 1, :] = jnp.full((1, BLK), up_sq[e] + down_sq[e])
    sq_send(0)
    ri.step(3)
    sq_sum(0)
    sq_send(1)
    ri.step(4)
    sq_sum(1)
    sq_send(2)
    ri.last()
    sq_sum(2)

    for e in range(EX):
        total = sq_a[e : e + 1, :]
        bound = clip[e].astype(F32) * BOUND
        f = jnp.minimum(1.0, bound / jnp.sqrt(total + 1e-6))[:, 0:1]
        n = SEQ // blk
        psc[e * SEQ : (e + 1) * SEQ] = (example(pg, e).astype(F32) * f).astype(BF16)
        at = slice(e * SEQ, (e + 1) * SEQ)
        csc[at] = (cotp[at].astype(F32) * f).astype(BF16)

    hf = hid[...].reshape(tokens, hidden)
    tile = 256
    outs = []
    for i in range(width // tile):
        at = slice(i * tile, (i + 1) * tile)
        g2 = dot(tokp[:, at], psc[...], 0, 0)
        for h in range(tile // BLK):
            lo = i * tile + h * BLK
            row = mu[lo // BLK : lo // BLK + 1, :] * UNIT
            uo[lo : lo + BLK, :] = (g2[h * BLK : (h + 1) * BLK] * row).astype(BF16)
        cp = pltpu.make_async_copy(uo.at[at], up_o.at[at], loc_sem.at[4 + i])
        cp.start()
        outs.append(cp)
    for i in range(hidden // tile):
        at = slice(i * tile, (i + 1) * tile)
        g2 = dot(hf[:, at], csc[...], 0, 0)
        for h in range(tile // BLK):
            lo = i * tile + h * BLK
            row = md[lo // BLK : lo // BLK + 1, :] * UNIT
            do[lo : lo + BLK, :] = (g2[h * BLK : (h + 1) * BLK] * row).astype(BF16)
        cp = pltpu.make_async_copy(do.at[at], dn_o.at[at], loc_sem.at[4 + width // tile + i])
        cp.start()
        outs.append(cp)
    ri.result(ing_o)
    for cp in outs:
        cp.wait()
    for copy in pending:
        copy.wait_send()


def solution(mesh):
    nz = mesh.shape["row"] // 4
    nc = mesh.shape["col"]

    def local(tok, cot, up, dn, upk, dnk, clip):
        width, hidden = up.shape
        tokens = tok.shape[0] * mesh.shape["row"]
        blk = tokens // nc
        half = nz // 2
        any_, vm, sm = (pl.BlockSpec(memory_space=m) for m in (pl.ANY, pltpu.VMEM, pltpu.SMEM))
        dma = pltpu.SemaphoreType.DMA
        n_ag = 1 + 4 * half + 2 * nz
        n_row = 3 + 2 * half
        return pl.pallas_call(
            functools.partial(kernel, nz, nc),
            out_shape=(
                jax.ShapeDtypeStruct(tok.shape, BF16),
                jax.ShapeDtypeStruct(tok.shape, BF16),
                jax.ShapeDtypeStruct(up.shape, BF16),
                jax.ShapeDtypeStruct(dn.shape, BF16),
            ),
            in_specs=[vm, vm, any_, any_, sm, sm, sm],
            out_specs=(vm, vm, any_, any_),
            scratch_shapes=[
                pltpu.VMEM((tokens, width), BF16),
                pltpu.VMEM((tokens, width), BF16),
                pltpu.VMEM((width, hidden), BF16),
                pltpu.VMEM((hidden, width), BF16),
                pltpu.VMEM((16, hidden), F32),
                pltpu.VMEM((8, width), F32),
                pltpu.VMEM((2, nc, blk, hidden), BF16),
                pltpu.VMEM((2, nc, blk, hidden), BF16),
                pltpu.VMEM((nc, blk, hidden), BF16),
                pltpu.VMEM((nc, blk, hidden), BF16),
                pltpu.VMEM((blk, hidden), F32),
                pltpu.VMEM((2, 2, nz, SUB, width), F32),
                pltpu.VMEM((2, 2, 2, nz, SUB, width), BF16),
                pltpu.VMEM((2, 2, nz, SUB, width), BF16),
                pltpu.VMEM((2, 2, half, 2, SUB, width), BF16),
                pltpu.VMEM((2, 2, half, 2, SUB, width), BF16),
                pltpu.VMEM((2, SUB, width), F32),
                pltpu.VMEM((2, 2, SUB, width), BF16),
                pltpu.VMEM((2, SUB, width), BF16),
                pltpu.VMEM((8, BLK), F32),
                pltpu.VMEM((3, 8, BLK), F32),
                pltpu.VMEM((3, 8, 8, BLK), F32),
                pltpu.VMEM((tokens, hidden), BF16),
                pltpu.VMEM((tokens, width), BF16),
                pltpu.VMEM((width, hidden), BF16),
                pltpu.VMEM((hidden, width), BF16),
                dma((16,)),
                dma((2, n_ag)),
                dma((2, n_ag)),
                dma((4, nc)),
                dma((4, nc)),
                dma((2, n_row)),
                dma((2, n_row)),
                dma((3, 8)),
                dma((3, 8)),
            ],
            compiler_params=pltpu.CompilerParams(
                collective_id=0, has_side_effects=True, vmem_limit_bytes=56 * 1024 * 1024
            ),
        )(tok, cot, up, dn, upk, dnk, clip)

    placed = (
        P("row", "col"),
        P("row", "col"),
        P("col", "row"),
        P("row", "col"),
        P("col", "row"),
        P("row", "col"),
        P(),
    )
    return jax.shard_map(
        local,
        mesh=mesh,
        in_specs=placed,
        out_specs=(P("row", "col"), P("row", "col"), P("col", "row"), P("row", "col")),
        check_vma=False,
    )
```

```python
import functools
import math

import jax
import jax.numpy as jnp
from jax import lax
from jax.experimental import pallas as pl
from jax.experimental.pallas import tpu as pltpu
from jax.sharding import PartitionSpec as P

MESH = pl.DeviceIdType.MESH
D = 12288
FF = 24576
SEQ = 128
BLK = 128
EX = 4
SUB = 16
F32 = jnp.float32
BF16 = jnp.bfloat16
ROOT = math.sqrt(2.0 / math.pi)
ROW_KEYS = [("x", 4), ("x", 3), ("x", -3), ("x", 2), ("x", -2), ("x", 0), ("n", 1), ("n", -1)]
ROW_KEYS += [("r", 4), ("r", 3), ("r", -3), ("z", 2), ("z", -2)]
UNIT = 7.0 / (EX * math.sqrt(SEQ))
BOUND = math.sqrt(D * FF * SEQ) / 1000.0


def dot(a, b, ca, cb):
    return lax.dot_general(a, b, (((ca,), (cb,)), ((), ())), preferred_element_type=F32)


def kernel(
    nz, nc,
    tok, cot, up, dn, upk, dnk, clip,
    out_o, ing_o, up_o, dn_o,
    tokp, cotp, upm, dnm, mu, md,
    send_h, recv_h, hid, pg, dact,
    part, pair, pair_r, row_out, row_in, near_out, near_in, fin, res,
    sq_a, sq_s, sq_r, psc, csc, uo, do,
    loc_sem, ag_s, ag_r, col_s, col_r, row_s, row_r, sq_ss, sq_rs,
):
    tokens = tok.shape[0] * 4 * nz
    width = tok.shape[1]
    hidden = up.shape[1]
    r = lax.axis_index("row")
    c = lax.axis_index("col")
    core = lax.rem(r, 2)
    z = lax.rem(lax.div(r, 2), nz)
    x = lax.div(r, 2 * nz)

    def row_of(xx, zz, kk):
        return (xx * nz + zz) * 2 + kk

    def zmod(v):
        return lax.rem(v + 2 * nz, nz)

    core_dev = (row_of(x, z, 1 - core), c)
    x_dev = (row_of(1 - x, z, core), c)

    def z_at(k):
        return (row_of(x, zmod(z + k), core), c)

    def c_at(k):
        return (r, lax.rem(c + k, nc))

    up_in = pltpu.make_async_copy(up, upm, loc_sem.at[0])
    dn_in = pltpu.make_async_copy(dn, dnm, loc_sem.at[1])
    up_in.start()
    dn_in.start()

    def rows(ref, xx, zz, kk):
        return ref.at[pl.ds(pl.multiple_of(row_of(xx, zz, kk) * SUB, SUB), SUB)]

    own = [
        pltpu.make_async_copy(tok, rows(tokp, x, z, core), loc_sem.at[2]),
        pltpu.make_async_copy(cot, rows(cotp, x, z, core), loc_sem.at[3]),
    ]
    own[0].start()
    own[1].start()

    barrier = pltpu.get_barrier_semaphore()
    near_c = [(0, 1)] + [(k, kk) for k in range(1, nc) for kk in (0, 1)]
    near_z = [(0, 1)] + [(k, m) for k in range(1, nz) for m in (0, 1)]

    def cc_at(k, kk):
        return (row_of(x, z, core if kk == 0 else 1 - core), lax.rem(c + k, nc))

    def xz_at(k, m):
        return (row_of(x if m == 0 else 1 - x, zmod(z + k), core), c)

    peers = [cc_at(*p) for p in near_c] + [xz_at(*p) for p in near_z]
    for dev in peers:
        pl.semaphore_signal(barrier, inc=1, device_id=dev, device_id_type=MESH)
    pl.semaphore_wait(barrier, len(peers))
    own[0].wait()
    own[1].wait()

    pending = []

    def send(src, dst, ssem, rsem, dev):
        copy = pltpu.make_async_remote_copy(
            src_ref=src, dst_ref=dst, send_sem=ssem, recv_sem=rsem, device_id=dev, device_id_type=MESH
        )
        copy.start()
        pending.append(copy)
        return copy

    def arrived(dst, rsem, dev):
        pltpu.make_async_remote_copy(
            src_ref=dst, dst_ref=dst, send_sem=rsem, recv_sem=rsem, device_id=dev, device_id_type=MESH
        ).wait_recv()

    class Gather:
        def __init__(self, a, shard, panel):
            self.a, self.shard, self.panel, self.keys = a, shard, panel, {}

        def sems(self, key):
            k = self.keys.setdefault(key, len(self.keys))
            return ag_s.at[self.a, k], ag_r.at[self.a, k]

        def slot(self, stream, off, kk=None):
            xx = x if stream == 0 else 1 - x
            return rows(self.panel, xx, zmod(z + off), core if kk is None else kk)

        def put(self, stream, off, key, dev):
            ref = self.slot(stream, off)
            send(ref, ref, *self.sems(key), dev)

        def take(self, stream, off, key):
            arrived(self.slot(stream, off), self.sems(key)[1], x_dev)

        def core_put(self, stream, off):
            self.put(stream, off, ("core", stream, off % nz), core_dev)

        def x_put(self, off):
            self.put(0, off, ("x", off % nz), x_dev)

        def start(self):
            for way, sign in ((0, 1), (1, -1)):
                self.put(0, 0, ("z", 0, sign), z_at(sign))
                self.put(0, 0, ("z", 0, 2 * sign), z_at(2 * sign))
            self.x_put(0)
            self.core_put(0, 0)

        def partner(self):
            self.take(1, 0, ("x", 0))
            for sign in (1, -1):
                self.put(1, 0, ("z", 1, sign), z_at(sign))
            self.core_put(1, 0)

        def near(self):
            for sign in (1, -1):
                self.take(0, -2 * sign, ("z", 0, 2 * sign))
                self.put(0, -2 * sign, ("z", 0, 3 * sign), z_at(sign))
                if sign == (1, -1)[self.a]:
                    self.put(0, -2 * sign, ("z", 0, 4), z_at(2 * sign))
                self.x_put(-2 * sign)
                self.core_put(0, -2 * sign)
            for sign in (1, -1):
                self.take(0, -sign, ("z", 0, sign))
                self.core_put(0, -sign)

        def far(self):
            for sign in (1, -1):
                self.take(0, -3 * sign, ("z", 0, 3 * sign))
                self.x_put(-3 * sign)
                self.core_put(0, -3 * sign)
            self.take(0, 4, ("z", 0, 4))
            self.x_put(4)
            self.core_put(0, 4)
            for sign in (1, -1):
                self.take(1, -sign, ("z", 1, sign))
                self.core_put(1, -sign)

        def finish(self):
            for off in (2, -2, 3, -3, 4):
                self.take(1, off, ("x", off % nz))
                self.core_put(1, off)
            for stream in (0, 1):
                for off in range(nz):
                    key = ("core", stream, off)
                    arrived(self.slot(stream, off, 1 - core), self.sems(key)[1], core_dev)

    gt = Gather(0, tok, tokp)
    gc = Gather(1, cot, cotp)
    gt.start()
    gt.partner()
    gt.near()
    gc.start()

    nbu, nbh = width // BLK, hidden // BLK
    for i in range(nbu):
        for j in range(nbh):
            mu[i : i + 1, j * BLK : (j + 1) * BLK] = jnp.full((1, BLK), upk[j, i].astype(F32))
            md[j : j + 1, i * BLK : (i + 1) * BLK] = jnp.full((1, BLK), dnk[j, i].astype(F32))
    up_in.wait()

    @pl.loop(0, nbu)
    def _(i):
        at = pl.ds(pl.multiple_of(i * BLK, BLK), BLK)
        upm[at, :] = upm[at, :] * mu[pl.ds(i, 1), :].astype(BF16)

    gt.far()
    gc.partner()
    dn_in.wait()

    @pl.loop(0, nbh)
    def _(j):
        at = pl.ds(pl.multiple_of(j * BLK, BLK), BLK)
        dnm[at, :] = dnm[at, :] * md[pl.ds(j, 1), :].astype(BF16)

    gc.near()
    gt.finish()

    blk = tokens // nc
    chunk = 256
    per = chunk // blk
    n_chunk = tokens // chunk

    def col_send(a, src, dst, q, k):
        return send(src, dst, col_s.at[a, k], col_r.at[a, k], (r, q))

    def scatter_chunk(a, m, value):
        for b in range(per):
            send_h[a, m * per + b] = value[b * blk : (b + 1) * blk].astype(BF16)

    def scatter_send(a):
        for k in range(1, nc):
            q = lax.rem(c + k, nc)
            col_send(a, send_h.at[a, q], recv_h.at[a, k], q, k)

    def scatter_sum(a):
        total = send_h[a, c].astype(F32)
        for k in range(1, nc):
            arrived(recv_h.at[a, k], col_r.at[a, k], c_at(nc - k))
            total += recv_h[a, k].astype(F32)
        return total

    def gather_send(a, panel):
        for k in range(1, nc):
            col_send(a, panel.at[c], panel.at[c], lax.rem(c + k, nc), k)

    def gather_wait(a, panel):
        for k in range(1, nc):
            q = lax.rem(c + nc - k, nc)
            arrived(panel.at[q], col_r.at[a, k], (r, q))

    for m in range(n_chunk):
        scatter_chunk(0, m, dot(tokp[m * chunk : (m + 1) * chunk], upm[...], 1, 0))
    scatter_send(0)

    gc.far()
    gc.finish()

    for m in range(n_chunk):
        scatter_chunk(1, m, dot(cotp[m * chunk : (m + 1) * chunk], dnm[...], 1, 1))
    scatter_send(1)

    v = scatter_sum(0)
    t = jnp.tanh(ROOT * (v + 0.044715 * (v * v * v)))
    hid[c] = (0.5 * v * (1.0 + t)).astype(BF16)
    gather_send(2, hid)
    dact[...] = 0.5 * (1.0 + t) + (0.5 * ROOT) * v * (1.0 - t * t) * (1.0 + 0.134145 * (v * v))

    g = scatter_sum(1)
    pg[c] = (g * dact[...]).astype(BF16)
    gather_send(3, pg)

    outs = []

    class RowSum:
        def __init__(self, a):
            self.a = a

        def sems(self, k):
            return row_s.at[self.a, k], row_r.at[self.a, k]

        def rows_of(self, m, value):
            v4 = value.reshape(nz, 2, SUB, width)
            part[self.a, 0, m] = v4[:, 0]
            part[self.a, 1, m] = v4[:, 1]
            pair[self.a, 0, m] = v4[:, 0].astype(BF16)
            pair[self.a, 1, m] = v4[:, 1].astype(BF16)
            send(pair.at[self.a, 1 - core, m], pair_r.at[self.a, m], *self.sems(m), core_dev)

        def pair_wait(self, m):
            arrived(pair_r.at[self.a, m], self.sems(m)[1], core_dev)

        def q(self, m, zz):
            return part[self.a, core, m, zz] + pair_r[self.a, m, zz].astype(F32)

        def key(self, name):
            return self.sems(2 + ROW_KEYS.index(name))

        def out(self, slot, name, dev):
            send(row_out.at[self.a, slot], row_in.at[self.a, slot], *self.key(name), dev)

        def get(self, slot, name):
            arrived(row_in.at[self.a, slot], self.key(name)[1], x_dev)

        def along_x(self):
            for slot, off in enumerate((4, 3, -3, 2, -2)):
                row_out[self.a, slot] = self.q(1 - x, zmod(z + off)).astype(BF16)
                self.out(slot, ("x", off), x_dev)
            for way, sign in ((0, 1), (1, -1)):
                for m in (0, 1):
                    near_out[self.a, way, m] = self.q(m, zmod(z + sign)).astype(BF16)
                send(near_out.at[self.a, way], near_in.at[self.a, way], *self.key(("n", sign)), z_at(sign))

        def relay(self):
            sign = (1, -1)[self.a]
            for slot, off, hop in ((0, 4, 2 * sign), (1, 3, 1), (2, -3, -1)):
                self.get(slot, ("x", off))
                val = self.q(x, zmod(z + off)) + row_in[self.a, slot].astype(F32)
                row_out[self.a, 5 + slot] = val.astype(BF16)
                self.out(5 + slot, ("r", off), z_at(hop))

        def near(self):
            for way, sign in ((0, 1), (1, -1)):
                arrived(near_in.at[self.a, way], self.key(("n", sign))[1], x_dev)
            for m in (0, 1):
                val = self.q(m, z)
                for way in (0, 1):
                    val += near_in[self.a, way, m].astype(F32)
                fin[self.a, m] = val
            row_out[self.a, 10] = fin[self.a, 1 - x].astype(BF16)
            self.out(10, ("x", 0), x_dev)

        def along_z(self):
            for way, sign in ((0, 1), (1, -1)):
                self.get(3 + way, ("x", 2 * sign))
                self.get(6 + way, ("r", 3 * sign))
                val = self.q(x, zmod(z + 2 * sign)) + row_in[self.a, 3 + way].astype(F32)
                val += row_in[self.a, 6 + way].astype(F32)
                if way == self.a:
                    self.get(5, ("r", 4))
                    val += row_in[self.a, 5].astype(F32)
                row_out[self.a, 8 + way] = val.astype(BF16)
                self.out(8 + way, ("z", 2 * sign), z_at(2 * sign))

        def result(self, o, sem):
            self.get(10, ("x", 0))
            val = fin[self.a, x] + row_in[self.a, 10].astype(F32)
            for way, sign in ((0, 1), (1, -1)):
                self.get(8 + way, ("z", 2 * sign))
                val += row_in[self.a, 8 + way].astype(F32)
            res[self.a] = val.astype(BF16)
            cp = pltpu.make_async_copy(res.at[self.a], o, sem)
            cp.start()
            outs.append(cp)

    def flat(ref, m):
        per_m = chunk // blk
        return ref[m * per_m : (m + 1) * per_m].reshape(chunk, hidden)

    def example(ref, e):
        n = SEQ // blk
        return ref[e * n : (e + 1) * n].reshape(SEQ, hidden)

    def norm_down(e):
        cote = cotp[e * SEQ : (e + 1) * SEQ]
        he = example(hid, e)
        acc = jnp.zeros((1, width), F32)
        for j in range(nbh):
            gg = dot(he[:, j * BLK : (j + 1) * BLK], cote, 0, 0)
            acc += jnp.sum(gg * gg, axis=0, keepdims=True) * md[j : j + 1, :]
        return jnp.sum(acc)

    def norm_up(e):
        toke = tokp[e * SEQ : (e + 1) * SEQ]
        pge = example(pg, e)
        acc = jnp.zeros((1, hidden), F32)
        for i in range(nbu):
            gg = dot(toke[:, i * BLK : (i + 1) * BLK], pge, 0, 0)
            acc += jnp.sum(gg * gg, axis=0, keepdims=True) * mu[i : i + 1, :]
        return jnp.sum(acc)

    groups = [
        [(cc_at(k, kk), cc_at(nc - k, kk)) for k, kk in near_c],
        [(xz_at(k, m), xz_at(nz - k, m)) for k, m in near_z],
    ]

    def sq_send(g):
        sq_s[g] = sq_a[...]
        for k, (dev, _) in enumerate(groups[g]):
            send(sq_s.at[g], sq_r.at[g, k], sq_ss.at[g, k], sq_rs.at[g, k], dev)

    def sq_sum(g):
        total = sq_a[...]
        for k, (_, dev) in enumerate(groups[g]):
            arrived(sq_r.at[g, k], sq_rs.at[g, k], dev)
            total += sq_r[g, k]
        sq_a[...] = total

    tile = 256

    def scale():
        for e in range(EX):
            total = sq_a[e : e + 1, :]
            bound = clip[e].astype(F32) * BOUND
            f = jnp.minimum(1.0, bound / jnp.sqrt(total + 1e-6))[:, 0:1]
            psc[e * SEQ : (e + 1) * SEQ] = (example(pg, e).astype(F32) * f).astype(BF16)
            at = slice(e * SEQ, (e + 1) * SEQ)
            csc[at] = (cotp[at].astype(F32) * f).astype(BF16)

    def update_up():
        for i in range(width // tile):
            at = slice(i * tile, (i + 1) * tile)
            g2 = dot(tokp[:, at], psc[...], 0, 0)
            for h in range(tile // BLK):
                lo = i * tile + h * BLK
                row = mu[lo // BLK : lo // BLK + 1, :] * UNIT
                uo[lo : lo + BLK, :] = (g2[h * BLK : (h + 1) * BLK] * row).astype(BF16)
            cp = pltpu.make_async_copy(uo.at[at], up_o.at[at], loc_sem.at[6 + i])
            cp.start()
            outs.append(cp)

    def update_down():
        hf = hid[...].reshape(tokens, hidden)
        for i in range(hidden // tile):
            at = slice(i * tile, (i + 1) * tile)
            g2 = dot(hf[:, at], csc[...], 0, 0)
            for h in range(tile // BLK):
                lo = i * tile + h * BLK
                row = md[lo // BLK : lo // BLK + 1, :] * UNIT
                do[lo : lo + BLK, :] = (g2[h * BLK : (h + 1) * BLK] * row).astype(BF16)
            cp = pltpu.make_async_copy(do.at[at], dn_o.at[at], loc_sem.at[6 + width // tile + i])
            cp.start()
            outs.append(cp)

    ro, ri = RowSum(0), RowSum(1)
    gather_wait(2, hid)
    for m in range(2):
        ro.rows_of(m, dot(flat(hid, m), dnm[...], 1, 0))
    down_sq = [norm_down(e) for e in range(EX)]
    ro.pair_wait(0)
    ro.pair_wait(1)
    ro.along_x()
    ro.relay()
    ro.near()

    gather_wait(3, pg)
    for m in range(2):
        ri.rows_of(m, dot(flat(pg, m), upm[...], 1, 1))
    sq_a[...] = jnp.zeros_like(sq_a)
    for e in range(EX):
        sq_a[e : e + 1, :] = jnp.full((1, BLK), norm_up(e) + down_sq[e])
    sq_send(0)
    ro.along_z()
    ri.pair_wait(0)
    ri.pair_wait(1)
    ri.along_x()
    ri.relay()
    sq_sum(0)
    sq_send(1)
    ro.result(out_o, loc_sem.at[4])
    ri.near()
    ri.along_z()
    sq_sum(1)
    scale()
    update_up()
    update_down()
    ri.result(ing_o, loc_sem.at[5])
    for cp in outs:
        cp.wait()
    for copy in pending:
        copy.wait_send()


def settle(*refs):
    sem = refs[-1]
    copies = []
    for i in range(4):
        src, dst = refs[i], refs[4 + i]
        pieces = 1 if src.shape[0] < 64 else 6
        step = src.shape[0] // pieces
        for p in range(pieces):
            at = pl.ds(p * step, step)
            copies.append(pltpu.make_async_copy(src.at[at], dst.at[at], sem.at[len(copies)]))
    for cp in copies:
        cp.start()
    for cp in copies:
        cp.wait()


def solution(mesh):
    nz = mesh.shape["row"] // 4
    nc = mesh.shape["col"]

    def local(tok, cot, up, dn, upk, dnk, clip):
        width, hidden = up.shape
        tokens = tok.shape[0] * mesh.shape["row"]
        blk = tokens // nc
        any_, vm, sm = (pl.BlockSpec(memory_space=m) for m in (pl.ANY, pltpu.VMEM, pltpu.SMEM))
        dma = pltpu.SemaphoreType.DMA
        n_ag = 32
        n_row = 2 + len(ROW_KEYS)
        shapes = (
            jax.ShapeDtypeStruct(tok.shape, BF16),
            jax.ShapeDtypeStruct(tok.shape, BF16),
            jax.ShapeDtypeStruct(up.shape, BF16),
            jax.ShapeDtypeStruct(dn.shape, BF16),
        )
        made = pl.pallas_call(
            functools.partial(kernel, nz, nc),
            out_shape=shapes,
            in_specs=[any_] * 4 + [sm] * 3,
            out_specs=(any_,) * 4,
            scratch_shapes=[
                pltpu.VMEM((tokens, width), BF16),
                pltpu.VMEM((tokens, width), BF16),
                pltpu.VMEM((width, hidden), BF16),
                pltpu.VMEM((hidden, width), BF16),
                pltpu.VMEM((16, hidden), F32),
                pltpu.VMEM((8, width), F32),
                pltpu.VMEM((2, nc, blk, hidden), BF16),
                pltpu.VMEM((2, nc, blk, hidden), BF16),
                pltpu.VMEM((nc, blk, hidden), BF16),
                pltpu.VMEM((nc, blk, hidden), BF16),
                pltpu.VMEM((blk, hidden), F32),
                pltpu.VMEM((2, 2, 2, nz, SUB, width), F32),
                pltpu.VMEM((2, 2, 2, nz, SUB, width), BF16),
                pltpu.VMEM((2, 2, nz, SUB, width), BF16),
                pltpu.VMEM((2, 11, SUB, width), BF16),
                pltpu.VMEM((2, 11, SUB, width), BF16),
                pltpu.VMEM((2, 2, 2, SUB, width), BF16),
                pltpu.VMEM((2, 2, 2, SUB, width), BF16),
                pltpu.VMEM((2, 2, SUB, width), F32),
                pltpu.VMEM((2, SUB, width), BF16),
                pltpu.VMEM((8, BLK), F32),
                pltpu.VMEM((2, 8, BLK), F32),
                pltpu.VMEM((2, 16, 8, BLK), F32),
                pltpu.VMEM((tokens, hidden), BF16),
                pltpu.VMEM((tokens, width), BF16),
                pltpu.VMEM((width, hidden), BF16),
                pltpu.VMEM((hidden, width), BF16),
                dma((24,)),
                dma((2, n_ag)),
                dma((2, n_ag)),
                dma((4, nc)),
                dma((4, nc)),
                dma((2, n_row)),
                dma((2, n_row)),
                dma((2, 16)),
                dma((2, 16)),
            ],
            compiler_params=pltpu.CompilerParams(
                collective_id=0, has_side_effects=True, vmem_limit_bytes=56 * 1024 * 1024
            ),
        )(tok, cot, up, dn, upk.T, dnk, clip)
        return pl.pallas_call(
            settle,
            out_shape=shapes,
            in_specs=[any_] * 4,
            out_specs=(any_,) * 4,
            scratch_shapes=[dma((16,))],
            compiler_params=pltpu.CompilerParams(vmem_limit_bytes=60 * 1024 * 1024),
        )(*made)

    placed = (
        P("row", "col"),
        P("row", "col"),
        P("col", "row"),
        P("row", "col"),
        P("col", "row"),
        P("row", "col"),
        P(),
    )
    return jax.shard_map(
        local,
        mesh=mesh,
        in_specs=placed,
        out_specs=(P("row", "col"), P("row", "col"), P("col", "row"), P("row", "col")),
        check_vma=False,
    )
```

```python
import functools
import math

import jax
import jax.numpy as jnp
from jax import lax
from jax.experimental import pallas as pl
from jax.experimental.pallas import tpu as pltpu
from jax.sharding import PartitionSpec as P

MESH = pl.DeviceIdType.MESH
D = 12288
FF = 24576
SEQ = 128
BLK = 128
EX = 4
SUB = 16
F32 = jnp.float32
BF16 = jnp.bfloat16
ROOT = math.sqrt(2.0 / math.pi)
ROW_KEYS = [("x", 4), ("x", 3), ("x", -3), ("x", 2), ("x", -2), ("x", 0), ("n", 1), ("n", -1)]
ROW_KEYS += [("r", 4), ("r", 3), ("r", -3), ("z", 2), ("z", -2)]
UNIT = 7.0 / (EX * math.sqrt(SEQ))
BOUND = math.sqrt(D * FF * SEQ) / 1000.0


def dot(a, b, ca, cb):
    return lax.dot_general(a, b, (((ca,), (cb,)), ((), ())), preferred_element_type=F32)


def kernel(
    nz, nc,
    tok, cot, up, dn, upk, dnk, clip,
    out_o, ing_o, up_o, dn_o,
    tokp, cotp, upm, dnm, mu, md,
    send_h, recv_h, hid, pg, dact,
    part, pair, pair_r, row_out, row_in, near_out, near_in, fin, res,
    sq_a, sq_s, sq_r, psc, csc, uo, do,
    loc_sem, ag_s, ag_r, col_s, col_r, row_s, row_r, sq_ss, sq_rs,
):
    tokens = tok.shape[0] * 4 * nz
    width = tok.shape[1]
    hidden = up.shape[1]
    r = lax.axis_index("row")
    c = lax.axis_index("col")
    core = lax.rem(r, 2)
    z = lax.rem(lax.div(r, 2), nz)
    x = lax.div(r, 2 * nz)

    def row_of(xx, zz, kk):
        return (xx * nz + zz) * 2 + kk

    def zmod(v):
        return lax.rem(v + 2 * nz, nz)

    core_dev = (row_of(x, z, 1 - core), c)
    x_dev = (row_of(1 - x, z, core), c)

    def z_at(k):
        return (row_of(x, zmod(z + k), core), c)

    def c_at(k):
        return (r, lax.rem(c + k, nc))

    up_in = pltpu.make_async_copy(up, upm, loc_sem.at[0])
    dn_in = pltpu.make_async_copy(dn, dnm, loc_sem.at[1])
    up_in.start()
    dn_in.start()

    def rows(ref, xx, zz, kk):
        return ref.at[pl.ds(pl.multiple_of(row_of(xx, zz, kk) * SUB, SUB), SUB)]

    own = [
        pltpu.make_async_copy(tok, rows(tokp, x, z, core), loc_sem.at[2]),
        pltpu.make_async_copy(cot, rows(cotp, x, z, core), loc_sem.at[3]),
    ]
    own[0].start()
    own[1].start()

    barrier = pltpu.get_barrier_semaphore()
    near_c = [(0, 1)] + [(k, kk) for k in range(1, nc) for kk in (0, 1)]
    near_z = [(0, 1)] + [(k, m) for k in range(1, nz) for m in (0, 1)]

    def cc_at(k, kk):
        return (row_of(x, z, core if kk == 0 else 1 - core), lax.rem(c + k, nc))

    def xz_at(k, m):
        return (row_of(x if m == 0 else 1 - x, zmod(z + k), core), c)

    peers = [cc_at(*p) for p in near_c] + [xz_at(*p) for p in near_z]
    for dev in peers:
        pl.semaphore_signal(barrier, inc=1, device_id=dev, device_id_type=MESH)
    pl.semaphore_wait(barrier, len(peers))
    own[0].wait()
    own[1].wait()

    pending = []

    def send(src, dst, ssem, rsem, dev):
        copy = pltpu.make_async_remote_copy(
            src_ref=src, dst_ref=dst, send_sem=ssem, recv_sem=rsem, device_id=dev, device_id_type=MESH
        )
        copy.start()
        pending.append(copy)
        return copy

    def arrived(dst, rsem, dev):
        pltpu.make_async_remote_copy(
            src_ref=dst, dst_ref=dst, send_sem=rsem, recv_sem=rsem, device_id=dev, device_id_type=MESH
        ).wait_recv()

    class Gather:
        def __init__(self, a, shard, panel):
            self.a, self.shard, self.panel, self.keys = a, shard, panel, {}

        def sems(self, key):
            k = self.keys.setdefault(key, len(self.keys))
            return ag_s.at[self.a, k], ag_r.at[self.a, k]

        def slot(self, stream, off, kk=None):
            xx = x if stream == 0 else 1 - x
            return rows(self.panel, xx, zmod(z + off), core if kk is None else kk)

        def put(self, stream, off, key, dev):
            ref = self.slot(stream, off)
            send(ref, ref, *self.sems(key), dev)

        def take(self, stream, off, key):
            arrived(self.slot(stream, off), self.sems(key)[1], x_dev)

        def core_put(self, stream, off):
            self.put(stream, off, ("core", stream, off % nz), core_dev)

        def x_put(self, off):
            self.put(0, off, ("x", off % nz), x_dev)

        def start(self):
            for way, sign in ((0, 1), (1, -1)):
                self.put(0, 0, ("z", 0, sign), z_at(sign))
                self.put(0, 0, ("z", 0, 2 * sign), z_at(2 * sign))
            self.x_put(0)
            self.core_put(0, 0)

        def partner(self):
            self.take(1, 0, ("x", 0))
            for sign in (1, -1):
                self.put(1, 0, ("z", 1, sign), z_at(sign))
            self.core_put(1, 0)

        def near(self):
            for sign in (1, -1):
                self.take(0, -2 * sign, ("z", 0, 2 * sign))
                self.put(0, -2 * sign, ("z", 0, 3 * sign), z_at(sign))
                if sign == (1, -1)[self.a]:
                    self.put(0, -2 * sign, ("z", 0, 4), z_at(2 * sign))
                self.x_put(-2 * sign)
                self.core_put(0, -2 * sign)
            for sign in (1, -1):
                self.take(0, -sign, ("z", 0, sign))
                self.core_put(0, -sign)

        def far(self):
            for sign in (1, -1):
                self.take(0, -3 * sign, ("z", 0, 3 * sign))
                self.x_put(-3 * sign)
                self.core_put(0, -3 * sign)
            self.take(0, 4, ("z", 0, 4))
            self.x_put(4)
            self.core_put(0, 4)
            for sign in (1, -1):
                self.take(1, -sign, ("z", 1, sign))
                self.core_put(1, -sign)

        def finish(self):
            for off in (2, -2, 3, -3, 4):
                self.take(1, off, ("x", off % nz))
                self.core_put(1, off)
            for stream in (0, 1):
                for off in range(nz):
                    key = ("core", stream, off)
                    arrived(self.slot(stream, off, 1 - core), self.sems(key)[1], core_dev)

    gt = Gather(0, tok, tokp)
    gc = Gather(1, cot, cotp)
    gt.start()
    gt.partner()
    gt.near()
    gc.start()

    nbu, nbh = width // BLK, hidden // BLK
    for i in range(nbu):
        for j in range(nbh):
            mu[i : i + 1, j * BLK : (j + 1) * BLK] = jnp.full((1, BLK), upk[j, i].astype(F32))
            md[j : j + 1, i * BLK : (i + 1) * BLK] = jnp.full((1, BLK), dnk[j, i].astype(F32))
    up_in.wait()

    @pl.loop(0, nbu)
    def _(i):
        at = pl.ds(pl.multiple_of(i * BLK, BLK), BLK)
        upm[at, :] = upm[at, :] * mu[pl.ds(i, 1), :].astype(BF16)

    gt.far()
    gc.partner()
    dn_in.wait()

    @pl.loop(0, nbh)
    def _(j):
        at = pl.ds(pl.multiple_of(j * BLK, BLK), BLK)
        dnm[at, :] = dnm[at, :] * md[pl.ds(j, 1), :].astype(BF16)

    gc.near()
    gt.finish()

    blk = tokens // nc
    chunk = 256
    per = chunk // blk
    n_chunk = tokens // chunk

    def col_send(a, src, dst, q, k):
        return send(src, dst, col_s.at[a, k], col_r.at[a, k], (r, q))

    def scatter_chunk(a, m, value):
        for b in range(per):
            send_h[a, m * per + b] = value[b * blk : (b + 1) * blk].astype(BF16)

    def scatter_send(a):
        for k in range(1, nc):
            q = lax.rem(c + k, nc)
            col_send(a, send_h.at[a, q], recv_h.at[a, k], q, k)

    def scatter_sum(a):
        total = send_h[a, c].astype(F32)
        for k in range(1, nc):
            arrived(recv_h.at[a, k], col_r.at[a, k], c_at(nc - k))
            total += recv_h[a, k].astype(F32)
        return total

    def gather_send(a, panel):
        for k in range(1, nc):
            col_send(a, panel.at[c], panel.at[c], lax.rem(c + k, nc), k)

    def gather_wait(a, panel):
        for k in range(1, nc):
            q = lax.rem(c + nc - k, nc)
            arrived(panel.at[q], col_r.at[a, k], (r, q))

    for m in range(n_chunk):
        scatter_chunk(0, m, dot(tokp[m * chunk : (m + 1) * chunk], upm[...], 1, 0))
    scatter_send(0)

    gc.far()
    gc.finish()

    for m in range(n_chunk):
        scatter_chunk(1, m, dot(cotp[m * chunk : (m + 1) * chunk], dnm[...], 1, 1))
    scatter_send(1)

    v = scatter_sum(0)
    t = jnp.tanh(ROOT * (v + 0.044715 * (v * v * v)))
    hid[c] = (0.5 * v * (1.0 + t)).astype(BF16)
    gather_send(2, hid)
    dact[...] = 0.5 * (1.0 + t) + (0.5 * ROOT) * v * (1.0 - t * t) * (1.0 + 0.134145 * (v * v))

    g = scatter_sum(1)
    pg[c] = (g * dact[...]).astype(BF16)
    gather_send(3, pg)

    outs = []

    class RowSum:
        def __init__(self, a):
            self.a = a

        def sems(self, k):
            return row_s.at[self.a, k], row_r.at[self.a, k]

        def rows_of(self, m, value):
            v4 = value.reshape(nz, 2, SUB, width)
            part[self.a, 0, m] = v4[:, 0]
            part[self.a, 1, m] = v4[:, 1]
            pair[self.a, 0, m] = v4[:, 0].astype(BF16)
            pair[self.a, 1, m] = v4[:, 1].astype(BF16)
            send(pair.at[self.a, 1 - core, m], pair_r.at[self.a, m], *self.sems(m), core_dev)

        def pair_wait(self, m):
            arrived(pair_r.at[self.a, m], self.sems(m)[1], core_dev)

        def q(self, m, zz):
            return part[self.a, core, m, zz] + pair_r[self.a, m, zz].astype(F32)

        def key(self, name):
            return self.sems(2 + ROW_KEYS.index(name))

        def out(self, slot, name, dev):
            send(row_out.at[self.a, slot], row_in.at[self.a, slot], *self.key(name), dev)

        def get(self, slot, name):
            arrived(row_in.at[self.a, slot], self.key(name)[1], x_dev)

        def along_x(self):
            for slot, off in enumerate((4, 3, -3, 2, -2)):
                row_out[self.a, slot] = self.q(1 - x, zmod(z + off)).astype(BF16)
                self.out(slot, ("x", off), x_dev)
            for way, sign in ((0, 1), (1, -1)):
                for m in (0, 1):
                    near_out[self.a, way, m] = self.q(m, zmod(z + sign)).astype(BF16)
                send(near_out.at[self.a, way], near_in.at[self.a, way], *self.key(("n", sign)), z_at(sign))

        def relay(self):
            sign = (1, -1)[self.a]
            for slot, off, hop in ((0, 4, 2 * sign), (1, 3, 1), (2, -3, -1)):
                self.get(slot, ("x", off))
                val = self.q(x, zmod(z + off)) + row_in[self.a, slot].astype(F32)
                row_out[self.a, 5 + slot] = val.astype(BF16)
                self.out(5 + slot, ("r", off), z_at(hop))

        def near(self):
            for way, sign in ((0, 1), (1, -1)):
                arrived(near_in.at[self.a, way], self.key(("n", sign))[1], x_dev)
            for m in (0, 1):
                val = self.q(m, z)
                for way in (0, 1):
                    val += near_in[self.a, way, m].astype(F32)
                fin[self.a, m] = val
            row_out[self.a, 10] = fin[self.a, 1 - x].astype(BF16)
            self.out(10, ("x", 0), x_dev)

        def along_z(self):
            for way, sign in ((0, 1), (1, -1)):
                self.get(3 + way, ("x", 2 * sign))
                self.get(6 + way, ("r", 3 * sign))
                val = self.q(x, zmod(z + 2 * sign)) + row_in[self.a, 3 + way].astype(F32)
                val += row_in[self.a, 6 + way].astype(F32)
                if way == self.a:
                    self.get(5, ("r", 4))
                    val += row_in[self.a, 5].astype(F32)
                row_out[self.a, 8 + way] = val.astype(BF16)
                self.out(8 + way, ("z", 2 * sign), z_at(2 * sign))

        def result(self, o, sem):
            self.get(10, ("x", 0))
            val = fin[self.a, x] + row_in[self.a, 10].astype(F32)
            for way, sign in ((0, 1), (1, -1)):
                self.get(8 + way, ("z", 2 * sign))
                val += row_in[self.a, 8 + way].astype(F32)
            res[self.a] = val.astype(BF16)
            cp = pltpu.make_async_copy(res.at[self.a], o, sem)
            cp.start()
            outs.append(cp)

    def flat(ref, m):
        per_m = chunk // blk
        return ref[m * per_m : (m + 1) * per_m].reshape(chunk, hidden)

    def example(ref, e):
        n = SEQ // blk
        return ref[e * n : (e + 1) * n].reshape(SEQ, hidden)

    def norm_down(e):
        cote = cotp[e * SEQ : (e + 1) * SEQ]
        he = example(hid, e)
        acc = jnp.zeros((1, width), F32)
        for j in range(nbh):
            gg = dot(he[:, j * BLK : (j + 1) * BLK], cote, 0, 0)
            acc += jnp.sum(gg * gg, axis=0, keepdims=True) * md[j : j + 1, :]
        return jnp.sum(acc)

    def norm_up(e):
        toke = tokp[e * SEQ : (e + 1) * SEQ]
        pge = example(pg, e)
        acc = jnp.zeros((1, hidden), F32)
        for i in range(nbu):
            gg = dot(toke[:, i * BLK : (i + 1) * BLK], pge, 0, 0)
            acc += jnp.sum(gg * gg, axis=0, keepdims=True) * mu[i : i + 1, :]
        return jnp.sum(acc)

    groups = [
        [(cc_at(k, kk), cc_at(nc - k, kk)) for k, kk in near_c],
        [(xz_at(k, m), xz_at(nz - k, m)) for k, m in near_z],
    ]

    def sq_send(g):
        sq_s[g] = sq_a[...]
        for k, (dev, _) in enumerate(groups[g]):
            send(sq_s.at[g], sq_r.at[g, k], sq_ss.at[g, k], sq_rs.at[g, k], dev)

    def sq_sum(g):
        total = sq_a[...]
        for k, (_, dev) in enumerate(groups[g]):
            arrived(sq_r.at[g, k], sq_rs.at[g, k], dev)
            total += sq_r[g, k]
        sq_a[...] = total

    tile = 256

    def scale():
        for e in range(EX):
            total = sq_a[e : e + 1, :]
            bound = clip[e].astype(F32) * BOUND
            f = jnp.minimum(1.0, bound / jnp.sqrt(total + 1e-6))[:, 0:1]
            psc[e * SEQ : (e + 1) * SEQ] = (example(pg, e).astype(F32) * f).astype(BF16)
            at = slice(e * SEQ, (e + 1) * SEQ)
            csc[at] = (cotp[at].astype(F32) * f).astype(BF16)

    def update_up():
        for i in range(width // tile):
            at = slice(i * tile, (i + 1) * tile)
            g2 = dot(tokp[:, at], psc[...], 0, 0)
            for h in range(tile // BLK):
                lo = i * tile + h * BLK
                row = mu[lo // BLK : lo // BLK + 1, :] * UNIT
                uo[lo : lo + BLK, :] = (g2[h * BLK : (h + 1) * BLK] * row).astype(BF16)
            cp = pltpu.make_async_copy(uo.at[at], up_o.at[at], loc_sem.at[6 + i])
            cp.start()
            outs.append(cp)

    def update_down():
        hf = hid[...].reshape(tokens, hidden)
        for i in range(hidden // tile):
            at = slice(i * tile, (i + 1) * tile)
            g2 = dot(hf[:, at], csc[...], 0, 0)
            for h in range(tile // BLK):
                lo = i * tile + h * BLK
                row = md[lo // BLK : lo // BLK + 1, :] * UNIT
                do[lo : lo + BLK, :] = (g2[h * BLK : (h + 1) * BLK] * row).astype(BF16)
            cp = pltpu.make_async_copy(do.at[at], dn_o.at[at], loc_sem.at[6 + width // tile + i])
            cp.start()
            outs.append(cp)

    ro, ri = RowSum(0), RowSum(1)
    gather_wait(2, hid)
    for m in range(2):
        ro.rows_of(m, dot(flat(hid, m), dnm[...], 1, 0))
    down_sq = [norm_down(e) for e in range(EX)]
    ro.pair_wait(0)
    ro.pair_wait(1)
    ro.along_x()

    gather_wait(3, pg)
    for m in range(2):
        ri.rows_of(m, dot(flat(pg, m), upm[...], 1, 1))
    sq_a[...] = jnp.zeros_like(sq_a)
    for e in range(EX):
        sq_a[e : e + 1, :] = jnp.full((1, BLK), norm_up(e) + down_sq[e])
    sq_send(0)
    ri.pair_wait(0)
    ri.pair_wait(1)
    ri.along_x()
    ro.relay()
    ro.near()
    ri.relay()
    ro.along_z()
    ri.near()
    sq_sum(0)
    sq_send(1)
    ri.along_z()
    ro.result(out_o, loc_sem.at[4])
    sq_sum(1)
    scale()
    update_up()
    update_down()
    ri.result(ing_o, loc_sem.at[5])
    for cp in outs:
        cp.wait()
    for copy in pending:
        copy.wait_send()


def settle(*refs):
    sem = refs[-1]
    moves = []
    for i in range(4):
        src, dst, held = refs[i], refs[4 + i], refs[8 + i]
        pieces = 1 if src.shape[0] < 64 else 6
        step = src.shape[0] // pieces
        for p in range(pieces):
            at, k = pl.ds(p * step, step), len(moves)
            moves.append(
                (
                    pltpu.make_async_copy(src.at[at], held.at[at], sem.at[0, k]),
                    pltpu.make_async_copy(held.at[at], dst.at[at], sem.at[1, k]),
                )
            )
    for get, _ in moves:
        get.start()
    for get, put in moves:
        get.wait()
        put.start()
    for _, put in moves:
        put.wait()


def solution(mesh):
    nz = mesh.shape["row"] // 4
    nc = mesh.shape["col"]

    def local(tok, cot, up, dn, upk, dnk, clip):
        width, hidden = up.shape
        tokens = tok.shape[0] * mesh.shape["row"]
        blk = tokens // nc
        any_, vm, sm = (pl.BlockSpec(memory_space=m) for m in (pl.ANY, pltpu.VMEM, pltpu.SMEM))
        dma = pltpu.SemaphoreType.DMA
        n_ag = 32
        n_row = 2 + len(ROW_KEYS)
        shapes = (
            jax.ShapeDtypeStruct(tok.shape, BF16),
            jax.ShapeDtypeStruct(tok.shape, BF16),
            jax.ShapeDtypeStruct(up.shape, BF16),
            jax.ShapeDtypeStruct(dn.shape, BF16),
        )
        made = pl.pallas_call(
            functools.partial(kernel, nz, nc),
            out_shape=shapes,
            in_specs=[any_] * 4 + [sm] * 3,
            out_specs=(any_,) * 4,
            scratch_shapes=[
                pltpu.VMEM((tokens, width), BF16),
                pltpu.VMEM((tokens, width), BF16),
                pltpu.VMEM((width, hidden), BF16),
                pltpu.VMEM((hidden, width), BF16),
                pltpu.VMEM((16, hidden), F32),
                pltpu.VMEM((8, width), F32),
                pltpu.VMEM((2, nc, blk, hidden), BF16),
                pltpu.VMEM((2, nc, blk, hidden), BF16),
                pltpu.VMEM((nc, blk, hidden), BF16),
                pltpu.VMEM((nc, blk, hidden), BF16),
                pltpu.VMEM((blk, hidden), F32),
                pltpu.VMEM((2, 2, 2, nz, SUB, width), F32),
                pltpu.VMEM((2, 2, 2, nz, SUB, width), BF16),
                pltpu.VMEM((2, 2, nz, SUB, width), BF16),
                pltpu.VMEM((2, 11, SUB, width), BF16),
                pltpu.VMEM((2, 11, SUB, width), BF16),
                pltpu.VMEM((2, 2, 2, SUB, width), BF16),
                pltpu.VMEM((2, 2, 2, SUB, width), BF16),
                pltpu.VMEM((2, 2, SUB, width), F32),
                pltpu.VMEM((2, SUB, width), BF16),
                pltpu.VMEM((8, BLK), F32),
                pltpu.VMEM((2, 8, BLK), F32),
                pltpu.VMEM((2, 16, 8, BLK), F32),
                pltpu.VMEM((tokens, hidden), BF16),
                pltpu.VMEM((tokens, width), BF16),
                pltpu.VMEM((width, hidden), BF16),
                pltpu.VMEM((hidden, width), BF16),
                dma((24,)),
                dma((2, n_ag)),
                dma((2, n_ag)),
                dma((4, nc)),
                dma((4, nc)),
                dma((2, n_row)),
                dma((2, n_row)),
                dma((2, 16)),
                dma((2, 16)),
            ],
            compiler_params=pltpu.CompilerParams(
                collective_id=0, has_side_effects=True, vmem_limit_bytes=56 * 1024 * 1024
            ),
        )(tok, cot, up, dn, upk.T, dnk, clip)
        return pl.pallas_call(
            settle,
            out_shape=shapes,
            in_specs=[any_] * 4,
            out_specs=(any_,) * 4,
            scratch_shapes=[pltpu.VMEM(t.shape, BF16) for t in shapes] + [dma((2, 16))],
            compiler_params=pltpu.CompilerParams(vmem_limit_bytes=60 * 1024 * 1024),
        )(*made)

    placed = (
        P("row", "col"),
        P("row", "col"),
        P("col", "row"),
        P("row", "col"),
        P("col", "row"),
        P("row", "col"),
        P(),
    )
    return jax.shard_map(
        local,
        mesh=mesh,
        in_specs=placed,
        out_specs=(P("row", "col"), P("row", "col"), P("col", "row"), P("row", "col")),
        check_vma=False,
    )
```

```python
import functools
import math

import jax
import jax.numpy as jnp
from jax import lax
from jax.experimental import pallas as pl
from jax.experimental.pallas import tpu as pltpu
from jax.sharding import PartitionSpec as P

MESH = pl.DeviceIdType.MESH
D = 12288
FF = 24576
SEQ = 128
BLK = 128
EX = 4
SUB = 16
F32 = jnp.float32
BF16 = jnp.bfloat16
ROOT = math.sqrt(2.0 / math.pi)
ROW_KEYS = [("x", 4), ("x", 3), ("x", -3), ("x", 2), ("x", -2), ("x", 0), ("n", 1), ("n", -1)]
ROW_KEYS += [("r", 4), ("r", 3), ("r", -3), ("z", 2), ("z", -2)]
UNIT = 7.0 / (EX * math.sqrt(SEQ))
BOUND = math.sqrt(D * FF * SEQ) / 1000.0


def dot(a, b, ca, cb):
    return lax.dot_general(a, b, (((ca,), (cb,)), ((), ())), preferred_element_type=F32)


def kernel(
    nz, nc,
    tok, cot, up, dn, upk, dnk,
    out_o, ing_o, tok_o, cot_o, hid_o, pg_o, mu_o, md_o, sq_o,
    tokp, cotp, upm, dnm, mu, md,
    send_h, via_x, via_y, from_x, from_y, sum_x, sum_y, hid, pg, dact,
    part, pair, pair_r, row_out, row_in, near_out, near_in, fin, res,
    sq_a, sq_s, sq_r,
    loc_sem, ag_s, ag_r, col_s, col_r, row_s, row_r, sq_ss, sq_rs,
):
    tokens = tok.shape[0] * 4 * nz
    width = tok.shape[1]
    hidden = up.shape[1]
    r = lax.axis_index("row")
    c = lax.axis_index("col")
    core = lax.rem(r, 2)
    z = lax.rem(lax.div(r, 2), nz)
    x = lax.div(r, 2 * nz)

    def row_of(xx, zz, kk):
        return (xx * nz + zz) * 2 + kk

    def zmod(v):
        return lax.rem(v + 2 * nz, nz)

    core_dev = (row_of(x, z, 1 - core), c)
    x_dev = (row_of(1 - x, z, core), c)

    def z_at(k):
        return (row_of(x, zmod(z + k), core), c)

    up_in = pltpu.make_async_copy(up, upm, loc_sem.at[0])
    dn_in = pltpu.make_async_copy(dn, dnm, loc_sem.at[1])
    up_in.start()
    dn_in.start()

    def rows(ref, xx, zz, kk):
        return ref.at[pl.ds(pl.multiple_of(row_of(xx, zz, kk) * SUB, SUB), SUB)]

    own = [
        pltpu.make_async_copy(tok, rows(tokp, x, z, core), loc_sem.at[2]),
        pltpu.make_async_copy(cot, rows(cotp, x, z, core), loc_sem.at[3]),
    ]
    own[0].start()
    own[1].start()

    barrier = pltpu.get_barrier_semaphore()
    near_c = [(0, 1)] + [(k, kk) for k in range(1, nc) for kk in (0, 1)]
    near_z = [(0, 1)] + [(k, m) for k in range(1, nz) for m in (0, 1)]

    def cc_at(k, kk):
        return (row_of(x, z, core if kk == 0 else 1 - core), lax.rem(c + k, nc))

    def xz_at(k, m):
        return (row_of(x if m == 0 else 1 - x, zmod(z + k), core), c)

    peers = [cc_at(*p) for p in near_c] + [xz_at(*p) for p in near_z]
    for dev in peers:
        pl.semaphore_signal(barrier, inc=1, device_id=dev, device_id_type=MESH)
    pl.semaphore_wait(barrier, len(peers))
    own[0].wait()
    own[1].wait()

    pending = []

    def send(src, dst, ssem, rsem, dev):
        copy = pltpu.make_async_remote_copy(
            src_ref=src, dst_ref=dst, send_sem=ssem, recv_sem=rsem, device_id=dev, device_id_type=MESH
        )
        copy.start()
        pending.append(copy)
        return copy

    def arrived(dst, rsem, dev):
        pltpu.make_async_remote_copy(
            src_ref=dst, dst_ref=dst, send_sem=rsem, recv_sem=rsem, device_id=dev, device_id_type=MESH
        ).wait_recv()

    class Gather:
        def __init__(self, a, shard, panel):
            self.a, self.shard, self.panel, self.keys = a, shard, panel, {}

        def sems(self, key):
            k = self.keys.setdefault(key, len(self.keys))
            return ag_s.at[self.a, k], ag_r.at[self.a, k]

        def slot(self, stream, off, kk=None):
            xx = x if stream == 0 else 1 - x
            return rows(self.panel, xx, zmod(z + off), core if kk is None else kk)

        def put(self, stream, off, key, dev):
            ref = self.slot(stream, off)
            send(ref, ref, *self.sems(key), dev)

        def take(self, stream, off, key):
            arrived(self.slot(stream, off), self.sems(key)[1], x_dev)

        def core_put(self, stream, off):
            self.put(stream, off, ("core", stream, off % nz), core_dev)

        def x_put(self, off):
            self.put(0, off, ("x", off % nz), x_dev)

        def start(self):
            for way, sign in ((0, 1), (1, -1)):
                self.put(0, 0, ("z", 0, sign), z_at(sign))
                self.put(0, 0, ("z", 0, 2 * sign), z_at(2 * sign))
            self.x_put(0)
            self.core_put(0, 0)

        def partner(self):
            self.take(1, 0, ("x", 0))
            for sign in (1, -1):
                self.put(1, 0, ("z", 1, sign), z_at(sign))
            self.core_put(1, 0)

        def near(self):
            for sign in (1, -1):
                self.take(0, -2 * sign, ("z", 0, 2 * sign))
                self.put(0, -2 * sign, ("z", 0, 3 * sign), z_at(sign))
                if sign == (1, -1)[self.a]:
                    self.put(0, -2 * sign, ("z", 0, 4), z_at(2 * sign))
                self.x_put(-2 * sign)
                self.core_put(0, -2 * sign)
            for sign in (1, -1):
                self.take(0, -sign, ("z", 0, sign))
                self.core_put(0, -sign)

        def far(self):
            for sign in (1, -1):
                self.take(0, -3 * sign, ("z", 0, 3 * sign))
                self.x_put(-3 * sign)
                self.core_put(0, -3 * sign)
            self.take(0, 4, ("z", 0, 4))
            self.x_put(4)
            self.core_put(0, 4)
            for sign in (1, -1):
                self.take(1, -sign, ("z", 1, sign))
                self.core_put(1, -sign)

        def finish(self):
            for off in (2, -2, 3, -3, 4):
                self.take(1, off, ("x", off % nz))
                self.core_put(1, off)
            for stream in (0, 1):
                for off in range(nz):
                    key = ("core", stream, off)
                    arrived(self.slot(stream, off, 1 - core), self.sems(key)[1], core_dev)

    gt = Gather(0, tok, tokp)
    gc = Gather(1, cot, cotp)
    gt.start()
    gt.partner()
    gt.near()
    gc.start()

    nbu, nbh = width // BLK, hidden // BLK
    for i in range(nbu):
        for j in range(nbh):
            mu[i : i + 1, j * BLK : (j + 1) * BLK] = jnp.full((1, BLK), upk[j, i].astype(F32))
            md[j : j + 1, i * BLK : (i + 1) * BLK] = jnp.full((1, BLK), dnk[j, i].astype(F32))
    up_in.wait()

    @pl.loop(0, nbu)
    def _(i):
        at = pl.ds(pl.multiple_of(i * BLK, BLK), BLK)
        upm[at, :] = upm[at, :] * mu[pl.ds(i, 1), :].astype(BF16)

    gt.far()
    gc.partner()
    dn_in.wait()

    @pl.loop(0, nbh)
    def _(j):
        at = pl.ds(pl.multiple_of(j * BLK, BLK), BLK)
        dnm[at, :] = dnm[at, :] * md[pl.ds(j, 1), :].astype(BF16)

    gc.near()
    gt.finish()

    blk = tokens // nc
    chunk = 256
    per = chunk // blk
    n_chunk = tokens // chunk

    low, high = pl.ds(0, blk // 2), pl.ds(blk // 2, blk // 2)
    ny = nc // 2
    y, xh = lax.div(c, 2), lax.rem(c, 2)
    ys = range(1, ny)

    def col(j, flip=0):
        return lax.rem(y + j + ny, ny) * 2 + (1 - xh if flip else xh)

    col_x = (r, col(0, 1))

    def col_y(j):
        return (r, col(j))

    class Col:
        def __init__(self, a):
            self.a, self.keys = a, {}

        def sems(self, key):
            k = self.keys.setdefault(key, len(self.keys))
            return col_s.at[self.a, k], col_r.at[self.a, k]

        def put(self, src, dst, key, dev):
            send(src, dst, *self.sems(key), dev)

        def take(self, dst, key):
            arrived(dst, self.sems(key)[1], col_x)

    class ColSum(Col):
        def chunk(self, m, value):
            for b in range(per):
                send_h[self.a, m * per + b] = value[b * blk : (b + 1) * blk].astype(BF16)

        def first(self):
            a = self.a
            for j in ys:
                self.put(send_h.at[a, col(j, 1), low], via_y.at[a, j], ("vy", j), col_y(j))
                self.put(send_h.at[a, col(j, 1), high], via_x.at[a, j], ("vx", j), col_x)
            for j in ys:
                self.put(send_h.at[a, col(j), low], from_y.at[a, j, low], ("oy", j), col_y(j))
            self.put(send_h.at[a, col(0, 1), high], from_x.at[a, high], "ox", col_x)

        def second(self):
            a = self.a
            for j in ys:
                self.take(via_x.at[a, j], ("vx", j))
                val = send_h[a, col(j), high, :].astype(F32) + via_x[a, j].astype(F32)
                sum_y[a, j] = val.astype(BF16)
                self.put(sum_y.at[a, j], from_y.at[a, j, high], ("sy", j), col_y(j))
            val = send_h[a, col(0, 1), low, :].astype(F32)
            for j in ys:
                self.take(via_y.at[a, j], ("vy", j))
                val += via_y[a, j].astype(F32)
            sum_x[a] = val.astype(BF16)
            self.put(sum_x.at[a], from_x.at[a, low], "sx", col_x)

        def total(self):
            a = self.a
            self.take(from_x.at[a, high], "ox")
            self.take(from_x.at[a, low], "sx")
            val = send_h[a, c].astype(F32) + from_x[a].astype(F32)
            for j in ys:
                self.take(from_y.at[a, j, low], ("oy", j))
                self.take(from_y.at[a, j, high], ("sy", j))
                val += from_y[a, j].astype(F32)
            return val

    class ColGather(Col):
        def __init__(self, a, panel):
            Col.__init__(self, a)
            self.panel = panel

        def first(self):
            own = self.panel.at[c]
            self.put(own, own, "x", col_x)
            for j in ys:
                self.put(own, own, ("y", j), col_y(j))

        def second(self):
            ref = self.panel.at[col(0, 1)]
            self.take(ref, "x")
            ref = self.panel.at[col(0, 1), low]
            for j in ys:
                self.put(ref, ref, ("xy", j), col_y(j))
            for j in ys:
                self.take(self.panel.at[col(-j)], ("y", j))
                ref = self.panel.at[col(-j), high]
                self.put(ref, ref, ("yx", j), col_x)

        def last(self):
            for j in ys:
                self.take(self.panel.at[col(-j, 1), low], ("xy", j))
                self.take(self.panel.at[col(-j, 1), high], ("yx", j))

    s_pre, s_grad = ColSum(0), ColSum(1)
    g_act, g_pre = ColGather(2, hid), ColGather(3, pg)
    keeps = []

    def keep(src, dst, k):
        cp = pltpu.make_async_copy(src, dst, loc_sem.at[8 + k])
        cp.start()
        keeps.append(cp)

    for m in range(n_chunk):
        s_pre.chunk(m, dot(tokp[m * chunk : (m + 1) * chunk], upm[...], 1, 0))
    s_pre.first()
    keep(tokp, tok_o, 0)
    keep(mu, mu_o, 1)
    keep(md, md_o, 2)

    gc.far()
    s_pre.second()
    gc.finish()
    keep(cotp, cot_o, 3)

    for m in range(n_chunk):
        s_grad.chunk(m, dot(cotp[m * chunk : (m + 1) * chunk], dnm[...], 1, 1))
    s_grad.first()

    v = s_pre.total()
    t = jnp.tanh(ROOT * (v + 0.044715 * (v * v * v)))
    hid[c] = (0.5 * v * (1.0 + t)).astype(BF16)
    g_act.first()
    dact[...] = 0.5 * (1.0 + t) + (0.5 * ROOT) * v * (1.0 - t * t) * (1.0 + 0.134145 * (v * v))

    s_grad.second()
    g_act.second()
    g = s_grad.total()
    pg[c] = (g * dact[...]).astype(BF16)
    g_pre.first()
    g_act.last()
    keep(hid, hid_o, 4)

    outs = []

    class RowSum:
        def __init__(self, a):
            self.a = a

        def sems(self, k):
            return row_s.at[self.a, k], row_r.at[self.a, k]

        def rows_of(self, m, value):
            v4 = value.reshape(nz, 2, SUB, width)
            part[self.a, 0, m] = v4[:, 0]
            part[self.a, 1, m] = v4[:, 1]
            pair[self.a, 0, m] = v4[:, 0].astype(BF16)
            pair[self.a, 1, m] = v4[:, 1].astype(BF16)
            send(pair.at[self.a, 1 - core, m], pair_r.at[self.a, m], *self.sems(m), core_dev)

        def pair_wait(self, m):
            arrived(pair_r.at[self.a, m], self.sems(m)[1], core_dev)

        def q(self, m, zz):
            return part[self.a, core, m, zz] + pair_r[self.a, m, zz].astype(F32)

        def key(self, name):
            return self.sems(2 + ROW_KEYS.index(name))

        def out(self, slot, name, dev):
            send(row_out.at[self.a, slot], row_in.at[self.a, slot], *self.key(name), dev)

        def get(self, slot, name):
            arrived(row_in.at[self.a, slot], self.key(name)[1], x_dev)

        def along_x(self):
            for slot, off in enumerate((4, 3, -3, 2, -2)):
                row_out[self.a, slot] = self.q(1 - x, zmod(z + off)).astype(BF16)
                self.out(slot, ("x", off), x_dev)
            for way, sign in ((0, 1), (1, -1)):
                for m in (0, 1):
                    near_out[self.a, way, m] = self.q(m, zmod(z + sign)).astype(BF16)
                send(near_out.at[self.a, way], near_in.at[self.a, way], *self.key(("n", sign)), z_at(sign))

        def relay(self):
            sign = (1, -1)[self.a]
            for slot, off, hop in ((0, 4, 2 * sign), (1, 3, 1), (2, -3, -1)):
                self.get(slot, ("x", off))
                val = self.q(x, zmod(z + off)) + row_in[self.a, slot].astype(F32)
                row_out[self.a, 5 + slot] = val.astype(BF16)
                self.out(5 + slot, ("r", off), z_at(hop))

        def near(self):
            for way, sign in ((0, 1), (1, -1)):
                arrived(near_in.at[self.a, way], self.key(("n", sign))[1], x_dev)
            for m in (0, 1):
                val = self.q(m, z)
                for way in (0, 1):
                    val += near_in[self.a, way, m].astype(F32)
                fin[self.a, m] = val
            row_out[self.a, 10] = fin[self.a, 1 - x].astype(BF16)
            self.out(10, ("x", 0), x_dev)

        def along_z(self):
            for way, sign in ((0, 1), (1, -1)):
                self.get(3 + way, ("x", 2 * sign))
                self.get(6 + way, ("r", 3 * sign))
                val = self.q(x, zmod(z + 2 * sign)) + row_in[self.a, 3 + way].astype(F32)
                val += row_in[self.a, 6 + way].astype(F32)
                if way == self.a:
                    self.get(5, ("r", 4))
                    val += row_in[self.a, 5].astype(F32)
                row_out[self.a, 8 + way] = val.astype(BF16)
                self.out(8 + way, ("z", 2 * sign), z_at(2 * sign))

        def result(self, o, sem):
            self.get(10, ("x", 0))
            val = fin[self.a, x] + row_in[self.a, 10].astype(F32)
            for way, sign in ((0, 1), (1, -1)):
                self.get(8 + way, ("z", 2 * sign))
                val += row_in[self.a, 8 + way].astype(F32)
            res[self.a] = val.astype(BF16)
            cp = pltpu.make_async_copy(res.at[self.a], o, sem)
            cp.start()
            outs.append(cp)

    def flat(ref, m):
        per_m = chunk // blk
        return ref[m * per_m : (m + 1) * per_m].reshape(chunk, hidden)

    def example(ref, e):
        n = SEQ // blk
        return ref[e * n : (e + 1) * n].reshape(SEQ, hidden)

    def norm_down(e):
        cote = cotp[e * SEQ : (e + 1) * SEQ]
        he = example(hid, e)
        acc = jnp.zeros((1, width), F32)
        for j in range(nbh):
            gg = dot(he[:, j * BLK : (j + 1) * BLK], cote, 0, 0)
            acc += jnp.sum(gg * gg, axis=0, keepdims=True) * md[j : j + 1, :]
        return jnp.sum(acc)

    def norm_up(e):
        toke = tokp[e * SEQ : (e + 1) * SEQ]
        pge = example(pg, e)
        acc = jnp.zeros((1, hidden), F32)
        for i in range(nbu):
            gg = dot(toke[:, i * BLK : (i + 1) * BLK], pge, 0, 0)
            acc += jnp.sum(gg * gg, axis=0, keepdims=True) * mu[i : i + 1, :]
        return jnp.sum(acc)

    groups = [
        [(cc_at(k, kk), cc_at(nc - k, kk)) for k, kk in near_c],
        [(xz_at(k, m), xz_at(nz - k, m)) for k, m in near_z],
    ]

    def sq_send(g):
        sq_s[g] = sq_a[...]
        for k, (dev, _) in enumerate(groups[g]):
            send(sq_s.at[g], sq_r.at[g, k], sq_ss.at[g, k], sq_rs.at[g, k], dev)

    def sq_sum(g):
        total = sq_a[...]
        for k, (_, dev) in enumerate(groups[g]):
            arrived(sq_r.at[g, k], sq_rs.at[g, k], dev)
            total += sq_r[g, k]
        sq_a[...] = total

    ro, ri = RowSum(0), RowSum(1)
    ro.rows_of(0, dot(flat(hid, 0), dnm[...], 1, 0))
    g_pre.second()
    ro.rows_of(1, dot(flat(hid, 1), dnm[...], 1, 0))
    down_sq = [norm_down(e) for e in range(EX)]
    ro.pair_wait(0)
    ro.pair_wait(1)
    ro.along_x()

    g_pre.last()
    keep(pg, pg_o, 5)
    for m in range(2):
        ri.rows_of(m, dot(flat(pg, m), upm[...], 1, 1))
    sq_a[...] = jnp.zeros_like(sq_a)
    for e in range(EX):
        sq_a[e : e + 1, :] = jnp.full((1, BLK), norm_up(e) + down_sq[e])
    sq_send(0)
    ri.pair_wait(0)
    ri.pair_wait(1)
    ri.along_x()
    ro.relay()
    ro.near()
    sq_sum(0)
    sq_send(1)
    ri.relay()
    ro.along_z()
    ri.near()
    ri.along_z()
    ro.result(out_o, loc_sem.at[4])
    sq_sum(1)
    keep(sq_a, sq_o, 6)
    ri.result(ing_o, loc_sem.at[5])
    for cp in outs + keeps:
        cp.wait()
    for copy in pending:
        copy.wait_send()


def update(
    out_t, ing_t, tok_t, cot_t, hid_t, pg_t, mu_t, md_t, sq_t, clip,
    out_o, ing_o, up_o, dn_o,
    out_v, ing_v, tokp, cotp, hid, pg, mu, md, sq, psc, csc, uo, do, sem, put_sem,
):
    def get(src, dst, k):
        cp = pltpu.make_async_copy(src, dst, sem.at[k])
        cp.start()
        return cp

    blk = hid_t.shape[1]
    tokens, width = tok_t.shape
    hidden = hid_t.shape[2]
    n = SEQ // blk
    got = [
        get(sq_t, sq, 0), get(pg_t, pg, 1), get(mu_t, mu, 2), get(md_t, md, 3),
        get(tok_t, tokp, 4), get(cot_t, cotp, 5), get(hid_t, hid, 6), get(out_t, out_v, 7), get(ing_t, ing_v, 8),
    ]
    puts = []

    def put(src, dst):
        cp = pltpu.make_async_copy(src, dst, put_sem.at[len(puts)])
        cp.start()
        puts.append(cp)

    got[0].wait()
    got[1].wait()
    scale = []
    for e in range(EX):
        bound = clip[e].astype(F32) * BOUND
        scale.append(jnp.minimum(1.0, bound / jnp.sqrt(sq[e : e + 1, :] + 1e-6))[:, 0:1])
        part = pg[e * n : (e + 1) * n].reshape(SEQ, hidden)
        psc[e * SEQ : (e + 1) * SEQ] = (part.astype(F32) * scale[e]).astype(BF16)
    for cp in got[2:5]:
        cp.wait()
    tile = 256
    for i in range(width // tile):
        at = slice(i * tile, (i + 1) * tile)
        g2 = dot(tokp[:, at], psc[...], 0, 0)
        for h in range(tile // BLK):
            lo = i * tile + h * BLK
            row = mu[lo // BLK : lo // BLK + 1, :] * UNIT
            uo[lo : lo + BLK, :] = (g2[h * BLK : (h + 1) * BLK] * row).astype(BF16)
        put(uo.at[at], up_o.at[at])
    for cp in got[5:]:
        cp.wait()
    put(out_v, out_o)
    put(ing_v, ing_o)
    for e in range(EX):
        at = slice(e * SEQ, (e + 1) * SEQ)
        csc[at] = (cotp[at].astype(F32) * scale[e]).astype(BF16)
    hf = hid[...].reshape(tokens, hidden)
    for i in range(hidden // tile):
        at = slice(i * tile, (i + 1) * tile)
        g2 = dot(hf[:, at], csc[...], 0, 0)
        for h in range(tile // BLK):
            lo = i * tile + h * BLK
            row = md[lo // BLK : lo // BLK + 1, :] * UNIT
            do[lo : lo + BLK, :] = (g2[h * BLK : (h + 1) * BLK] * row).astype(BF16)
        put(do.at[at], dn_o.at[at])
    for cp in puts:
        cp.wait()


def solution(mesh):
    nz = mesh.shape["row"] // 4
    nc = mesh.shape["col"]

    def local(tok, cot, up, dn, upk, dnk, clip):
        width, hidden = up.shape
        tokens = tok.shape[0] * mesh.shape["row"]
        blk = tokens // nc
        any_, vm, sm = (pl.BlockSpec(memory_space=m) for m in (pl.ANY, pltpu.VMEM, pltpu.SMEM))
        dma = pltpu.SemaphoreType.DMA
        n_ag = 32
        n_row = 2 + len(ROW_KEYS)
        panel = jax.ShapeDtypeStruct((tokens, width), BF16)
        rowed = jax.ShapeDtypeStruct((nc, blk, hidden), BF16)
        shard = jax.ShapeDtypeStruct(tok.shape, BF16)
        up_mask = jax.ShapeDtypeStruct((16, hidden), F32)
        down_mask = jax.ShapeDtypeStruct((8, width), F32)
        squares = jax.ShapeDtypeStruct((8, BLK), F32)
        made = pl.pallas_call(
            functools.partial(kernel, nz, nc),
            out_shape=(shard, shard, panel, panel, rowed, rowed, up_mask, down_mask, squares),
            in_specs=[any_] * 4 + [sm] * 2,
            out_specs=(any_,) * 9,
            scratch_shapes=[
                pltpu.VMEM((tokens, width), BF16),
                pltpu.VMEM((tokens, width), BF16),
                pltpu.VMEM((width, hidden), BF16),
                pltpu.VMEM((hidden, width), BF16),
                pltpu.VMEM((16, hidden), F32),
                pltpu.VMEM((8, width), F32),
                pltpu.VMEM((2, nc, blk, hidden), BF16),
                pltpu.VMEM((2, nc // 2, blk // 2, hidden), BF16),
                pltpu.VMEM((2, nc // 2, blk // 2, hidden), BF16),
                pltpu.VMEM((2, blk, hidden), BF16),
                pltpu.VMEM((2, nc // 2, blk, hidden), BF16),
                pltpu.VMEM((2, blk // 2, hidden), BF16),
                pltpu.VMEM((2, nc // 2, blk // 2, hidden), BF16),
                pltpu.VMEM((nc, blk, hidden), BF16),
                pltpu.VMEM((nc, blk, hidden), BF16),
                pltpu.VMEM((blk, hidden), F32),
                pltpu.VMEM((2, 2, 2, nz, SUB, width), F32),
                pltpu.VMEM((2, 2, 2, nz, SUB, width), BF16),
                pltpu.VMEM((2, 2, nz, SUB, width), BF16),
                pltpu.VMEM((2, 11, SUB, width), BF16),
                pltpu.VMEM((2, 11, SUB, width), BF16),
                pltpu.VMEM((2, 2, 2, SUB, width), BF16),
                pltpu.VMEM((2, 2, 2, SUB, width), BF16),
                pltpu.VMEM((2, 2, SUB, width), F32),
                pltpu.VMEM((2, SUB, width), BF16),
                pltpu.VMEM((8, BLK), F32),
                pltpu.VMEM((2, 8, BLK), F32),
                pltpu.VMEM((2, 16, 8, BLK), F32),
                dma((16,)),
                dma((2, n_ag)),
                dma((2, n_ag)),
                dma((4, 16)),
                dma((4, 16)),
                dma((2, n_row)),
                dma((2, n_row)),
                dma((2, 16)),
                dma((2, 16)),
            ],
            compiler_params=pltpu.CompilerParams(
                collective_id=0, has_side_effects=True, vmem_limit_bytes=56 * 1024 * 1024
            ),
        )(tok, cot, up, dn, upk.T, dnk)
        grad_up = jax.ShapeDtypeStruct(up.shape, BF16)
        grad_dn = jax.ShapeDtypeStruct(dn.shape, BF16)
        held = (shard, shard, panel, panel, rowed, rowed, up_mask, down_mask, squares)
        held += (jax.ShapeDtypeStruct((tokens, hidden), BF16), panel, grad_up, grad_dn)
        return pl.pallas_call(
            update,
            out_shape=(shard, shard, grad_up, grad_dn),
            in_specs=[any_] * 9 + [sm],
            out_specs=(any_,) * 4,
            scratch_shapes=[pltpu.VMEM(t.shape, t.dtype) for t in held] + [dma((16,)), dma((16,))],
            compiler_params=pltpu.CompilerParams(vmem_limit_bytes=60 * 1024 * 1024),
        )(*made, clip)

    placed = (
        P("row", "col"),
        P("row", "col"),
        P("col", "row"),
        P("row", "col"),
        P("col", "row"),
        P("row", "col"),
        P(),
    )
    return jax.shard_map(
        local,
        mesh=mesh,
        in_specs=placed,
        out_specs=(P("row", "col"), P("row", "col"), P("col", "row"), P("row", "col")),
        check_vma=False,
    )
```

```python
import functools
import math

import jax
import jax.numpy as jnp
from jax import lax
from jax.experimental import pallas as pl
from jax.experimental.pallas import tpu as pltpu
from jax.sharding import PartitionSpec as P

MESH = pl.DeviceIdType.MESH
D = 12288
FF = 24576
SEQ = 128
BLK = 128
EX = 4
SUB = 16
F32 = jnp.float32
BF16 = jnp.bfloat16
ROOT = math.sqrt(2.0 / math.pi)
ROW_KEYS = [("x", 4), ("x", 3), ("x", -3), ("x", 2), ("x", -2), ("x", 0), ("n", 1), ("n", -1)]
ROW_KEYS += [("r", 4), ("r", 3), ("r", -3), ("z", 2), ("z", -2)]
UNIT = 7.0 / (EX * math.sqrt(SEQ))
BOUND = math.sqrt(D * FF * SEQ) / 1000.0


def dot(a, b, ca, cb):
    return lax.dot_general(a, b, (((ca,), (cb,)), ((), ())), preferred_element_type=F32)


def kernel(
    nz, nc,
    tok, cot, up, dn, upk, dnk, clip,
    out_o, ing_o, tok_o, cot_o, hid_o, pg_o, mu_o, md_o, fac_o,
    tokp, cotp, upm, dnm, mu, md,
    send_h, via_x, via_y, from_x, from_y, sum_x, sum_y, hid, pg, dact,
    part, pair, pair_r, row_out, row_in, near_out, near_in, fin, res,
    sq_a, sq_s, sq_r, fac,
    loc_sem, ag_s, ag_r, col_s, col_r, row_s, row_r, sq_ss, sq_rs,
):
    tokens = tok.shape[0] * 4 * nz
    width = tok.shape[1]
    hidden = up.shape[1]
    r = lax.axis_index("row")
    c = lax.axis_index("col")
    core = lax.rem(r, 2)
    z = lax.rem(lax.div(r, 2), nz)
    x = lax.div(r, 2 * nz)

    def row_of(xx, zz, kk):
        return (xx * nz + zz) * 2 + kk

    def zmod(v):
        return lax.rem(v + 2 * nz, nz)

    core_dev = (row_of(x, z, 1 - core), c)
    x_dev = (row_of(1 - x, z, core), c)

    def z_at(k):
        return (row_of(x, zmod(z + k), core), c)

    up_in = pltpu.make_async_copy(up, upm, loc_sem.at[0])
    dn_in = pltpu.make_async_copy(dn, dnm, loc_sem.at[1])
    up_in.start()
    dn_in.start()

    def place(off):
        return (off + 1) % nz

    own = [
        pltpu.make_async_copy(tok, tokp.at[place(0), 0, 0], loc_sem.at[2]),
        pltpu.make_async_copy(cot, cotp.at[place(0), 0, 0], loc_sem.at[3]),
    ]
    own[0].start()
    own[1].start()

    barrier = pltpu.get_barrier_semaphore()
    near_c = [(0, 1)] + [(k, kk) for k in range(1, nc) for kk in (0, 1)]
    near_z = [(0, 1)] + [(k, m) for k in range(1, nz) for m in (0, 1)]

    def cc_at(k, kk):
        return (row_of(x, z, core if kk == 0 else 1 - core), lax.rem(c + k, nc))

    def xz_at(k, m):
        return (row_of(x if m == 0 else 1 - x, zmod(z + k), core), c)

    peers = [cc_at(*p) for p in near_c] + [xz_at(*p) for p in near_z]
    for dev in peers:
        pl.semaphore_signal(barrier, inc=1, device_id=dev, device_id_type=MESH)
    pl.semaphore_wait(barrier, len(peers))
    own[0].wait()
    own[1].wait()

    pending = []

    def send(src, dst, ssem, rsem, dev):
        copy = pltpu.make_async_remote_copy(
            src_ref=src, dst_ref=dst, send_sem=ssem, recv_sem=rsem, device_id=dev, device_id_type=MESH
        )
        copy.start()
        pending.append(copy)
        return copy

    def arrived(dst, rsem, dev):
        pltpu.make_async_remote_copy(
            src_ref=dst, dst_ref=dst, send_sem=rsem, recv_sem=rsem, device_id=dev, device_id_type=MESH
        ).wait_recv()

    class Gather:
        def __init__(self, a, shard, panel):
            self.a, self.shard, self.panel, self.keys = a, shard, panel, {}

        def sems(self, key):
            k = self.keys.setdefault(key, len(self.keys))
            return ag_s.at[self.a, k], ag_r.at[self.a, k]

        def slot(self, stream, off, other=0):
            return self.panel.at[place(off), stream, other]

        def z_put(self, stream, off, hop, key):
            src, dst = self.slot(stream, off), self.slot(stream, off - hop)
            send(src, dst, *self.sems(key), z_at(hop))

        def take(self, stream, off, key):
            arrived(self.slot(stream, off), self.sems(key)[1], x_dev)

        def core_put(self, stream, off):
            src, dst = self.slot(stream, off), self.slot(stream, off, 1)
            send(src, dst, *self.sems(("core", stream, off % nz)), core_dev)

        def x_put(self, off):
            send(self.slot(0, off), self.slot(1, off), *self.sems(("x", off % nz)), x_dev)

        def start(self):
            for sign in (1, -1):
                self.z_put(0, 0, sign, ("z", 0, sign))
                self.z_put(0, 0, 2 * sign, ("z", 0, 2 * sign))
            self.x_put(0)
            self.core_put(0, 0)

        def partner(self):
            self.take(1, 0, ("x", 0))
            for sign in (1, -1):
                self.z_put(1, 0, sign, ("z", 1, sign))
            self.core_put(1, 0)

        def near(self):
            for sign in (-1, 1):
                self.take(0, -2 * sign, ("z", 0, 2 * sign))
                self.x_put(-2 * sign)
                self.z_put(0, -2 * sign, sign, ("z", 0, 3 * sign))
                if sign == (1, -1)[self.a]:
                    self.z_put(0, -2 * sign, 2 * sign, ("z", 0, 4))
                self.core_put(0, -2 * sign)
            for sign in (1, -1):
                self.take(0, -sign, ("z", 0, sign))
                self.core_put(0, -sign)

        def near_done(self):
            for sign in (1, -1):
                self.take(1, -sign, ("z", 1, sign))
                self.core_put(1, -sign)
            self.take(1, 2, ("x", 2))
            self.core_put(1, 2)
            self.core_wait((-1, 0, 1, 2))

        def far(self):
            for sign in (1, -1):
                self.take(0, -3 * sign, ("z", 0, 3 * sign))
                self.x_put(-3 * sign)
                self.core_put(0, -3 * sign)
            self.take(0, 4, ("z", 0, 4))
            self.x_put(4)
            self.core_put(0, 4)

        def far_done(self):
            for off in (-2, 3, -3, 4):
                self.take(1, off, ("x", off % nz))
                self.core_put(1, off)
            self.core_wait((-2, 3, -3, 4))

        def core_wait(self, offs):
            for stream in (0, 1):
                for off in offs:
                    key = ("core", stream, off % nz)
                    arrived(self.slot(stream, off, 1), self.sems(key)[1], core_dev)

    gt = Gather(0, tok, tokp)
    gc = Gather(1, cot, cotp)
    gt.start()
    gt.partner()
    gt.near()
    gc.start()

    nbu, nbh = width // BLK, hidden // BLK
    for i in range(nbu):
        for j in range(nbh):
            mu[i : i + 1, j * BLK : (j + 1) * BLK] = jnp.full((1, BLK), upk[j, i].astype(F32))
            md[j : j + 1, i * BLK : (i + 1) * BLK] = jnp.full((1, BLK), dnk[j, i].astype(F32))
    up_in.wait()

    @pl.loop(0, nbu)
    def _(i):
        at = pl.ds(pl.multiple_of(i * BLK, BLK), BLK)
        upm[at, :] = upm[at, :] * mu[pl.ds(i, 1), :].astype(BF16)

    dn_in.wait()

    @pl.loop(0, nbh)
    def _(j):
        at = pl.ds(pl.multiple_of(j * BLK, BLK), BLK)
        dnm[at, :] = dnm[at, :] * md[pl.ds(j, 1), :].astype(BF16)

    chunk = tokens // 2
    blk = chunk // nc
    low, high = pl.ds(0, blk // 2), pl.ds(blk // 2, blk // 2)
    ny = nc // 2
    y, xh = lax.div(c, 2), lax.rem(c, 2)
    ys = range(1, ny)
    NEAR, FAR = 0, 1

    def half(ref, ch):
        n = nz // 2
        return ref[ch * n : (ch + 1) * n].reshape(chunk, ref.shape[-1])

    def col(j, flip=0):
        return lax.rem(y + j + ny, ny) * 2 + (1 - xh if flip else xh)

    col_x = (r, col(0, 1))

    def col_y(j):
        return (r, col(j))

    class Col:
        def __init__(self, a):
            self.a, self.keys = a, {}

        def sems(self, key):
            k = self.keys.setdefault(key, len(self.keys))
            return col_s.at[self.a, k], col_r.at[self.a, k]

        def put(self, src, dst, key, dev):
            send(src, dst, *self.sems(key), dev)

        def take(self, dst, key):
            arrived(dst, self.sems(key)[1], col_x)

    class ColSum(Col):
        def first(self, value):
            a = self.a
            for b in range(nc):
                send_h[a, b] = value[b * blk : (b + 1) * blk].astype(BF16)
            for j in ys:
                self.put(send_h.at[a, col(j, 1), low], via_y.at[a, j], ("vy", j), col_y(j))
                self.put(send_h.at[a, col(j, 1), high], via_x.at[a, j], ("vx", j), col_x)
            for j in ys:
                self.put(send_h.at[a, col(j), low], from_y.at[a, j, low], ("oy", j), col_y(j))
            self.put(send_h.at[a, col(0, 1), high], from_x.at[a, high], "ox", col_x)

        def second(self):
            a = self.a
            for j in ys:
                self.take(via_x.at[a, j], ("vx", j))
                val = send_h[a, col(j), high, :].astype(F32) + via_x[a, j].astype(F32)
                sum_y[a, j] = val.astype(BF16)
                self.put(sum_y.at[a, j], from_y.at[a, j, high], ("sy", j), col_y(j))
            val = send_h[a, col(0, 1), low, :].astype(F32)
            for j in ys:
                self.take(via_y.at[a, j], ("vy", j))
                val += via_y[a, j].astype(F32)
            sum_x[a] = val.astype(BF16)
            self.put(sum_x.at[a], from_x.at[a, low], "sx", col_x)

        def total(self):
            a = self.a
            self.take(from_x.at[a, high], "ox")
            self.take(from_x.at[a, low], "sx")
            val = send_h[a, c].astype(F32) + from_x[a].astype(F32)
            for j in ys:
                self.take(from_y.at[a, j, low], ("oy", j))
                self.take(from_y.at[a, j, high], ("sy", j))
                val += from_y[a, j].astype(F32)
            return val

    class ColGather(Col):
        def __init__(self, a, panel, ch):
            Col.__init__(self, a)
            self.panel, self.ch = panel, ch

        def block(self, q, part=None):
            at = (self.ch * (nz // 2) + lax.div(q, 2), lax.rem(q, 2))
            return self.panel.at[at] if part is None else self.panel.at[at + (part,)]

        def first(self, value):
            self.panel[self.ch * (nz // 2) + lax.div(c, 2), lax.rem(c, 2)] = value.astype(BF16)
            own = self.block(c)
            self.put(own, own, "x", col_x)
            for j in ys:
                self.put(own, own, ("y", j), col_y(j))

        def second(self):
            self.take(self.block(col(0, 1)), "x")
            ref = self.block(col(0, 1), low)
            for j in ys:
                self.put(ref, ref, ("xy", j), col_y(j))
            for j in ys:
                self.take(self.block(col(-j)), ("y", j))
                ref = self.block(col(-j), high)
                self.put(ref, ref, ("yx", j), col_x)

        def last(self):
            for j in ys:
                self.take(self.block(col(-j, 1), low), ("xy", j))
                self.take(self.block(col(-j, 1), high), ("yx", j))

    s_pre, s_grad = [ColSum(0), ColSum(1)], [ColSum(2), ColSum(3)]
    g_act = [ColGather(4, hid, NEAR), ColGather(5, hid, FAR)]
    g_pre = [ColGather(6, pg, NEAR), ColGather(7, pg, FAR)]
    keeps = []

    def keep(src, dst, k):
        cp = pltpu.make_async_copy(src, dst, loc_sem.at[8 + k])
        cp.start()
        keeps.append(cp)

    def activate(ch):
        v = s_pre[ch].total()
        t = jnp.tanh(ROOT * (v + 0.044715 * (v * v * v)))
        g_act[ch].first(0.5 * v * (1.0 + t))
        dact[ch] = 0.5 * (1.0 + t) + (0.5 * ROOT) * v * (1.0 - t * t) * (1.0 + 0.134145 * (v * v))

    gt.near_done()
    s_pre[NEAR].first(dot(half(tokp, NEAR), upm[...], 1, 0))
    gt.far()
    gc.partner()
    s_pre[NEAR].second()
    gt.far_done()
    s_pre[FAR].first(dot(half(tokp, FAR), upm[...], 1, 0))
    gc.near()
    keep(tokp, tok_o, 0)
    keep(mu, mu_o, 1)
    keep(md, md_o, 2)
    activate(NEAR)
    s_pre[FAR].second()
    gc.near_done()
    gc.far()
    gc.far_done()
    keep(cotp, cot_o, 3)
    s_grad[FAR].first(dot(half(cotp, FAR), dnm[...], 1, 1))
    s_grad[NEAR].first(dot(half(cotp, NEAR), dnm[...], 1, 1))
    g_act[NEAR].second()
    activate(FAR)
    s_grad[FAR].second()
    s_grad[NEAR].second()
    g_act[FAR].second()
    g_pre[FAR].first(s_grad[FAR].total() * dact[FAR])
    g_pre[NEAR].first(s_grad[NEAR].total() * dact[NEAR])

    outs = []

    class RowSum:
        def __init__(self, a):
            self.a = a

        def sems(self, k):
            return row_s.at[self.a, k], row_r.at[self.a, k]

        def emit(self, ch, value):
            n = nz // 2
            v5 = value.reshape(n, 2, 2, SUB, width)
            part[self.a, ch * n : (ch + 1) * n] = v5[:, :, 0]
            pair[self.a, ch * n : (ch + 1) * n] = v5[:, :, 1]
            at = pl.ds(ch * n, n)
            send(pair.at[self.a, at], pair_r.at[self.a, at], *self.sems(ch), core_dev)

        def pair_wait(self, ch):
            at = pl.ds(ch * (nz // 2), nz // 2)
            arrived(pair_r.at[self.a, at], self.sems(ch)[1], core_dev)

        def q(self, stream, off):
            return part[self.a, place(off), stream] + pair_r[self.a, place(off), stream]

        def key(self, name):
            return self.sems(2 + ROW_KEYS.index(name))

        def out(self, slot, name, dev):
            send(row_out.at[self.a, slot], row_in.at[self.a, slot], *self.key(name), dev)

        def get(self, slot, name):
            arrived(row_in.at[self.a, slot], self.key(name)[1], x_dev)

        def along_x(self, slots):
            for slot in slots:
                off = (4, 3, -3, 2, -2)[slot]
                row_out[self.a, slot] = self.q(1, off).astype(BF16)
                self.out(slot, ("x", off), x_dev)

        def next_door(self):
            for way, sign in ((0, 1), (1, -1)):
                for m in (0, 1):
                    near_out[self.a, way, m] = self.q(m, sign).astype(BF16)
                send(near_out.at[self.a, way], near_in.at[self.a, way], *self.key(("n", sign)), z_at(sign))

        def relay(self):
            sign = (1, -1)[self.a]
            for slot, off, hop in ((0, 4, 2 * sign), (1, 3, 1), (2, -3, -1)):
                self.get(slot, ("x", off))
                val = self.q(0, off) + row_in[self.a, slot].astype(F32)
                row_out[self.a, 5 + slot] = val.astype(BF16)
                self.out(5 + slot, ("r", off), z_at(hop))

        def near(self):
            for way, sign in ((0, 1), (1, -1)):
                arrived(near_in.at[self.a, way], self.key(("n", sign))[1], x_dev)
            for m in (0, 1):
                val = self.q(m, 0)
                for way in (0, 1):
                    val += near_in[self.a, way, m].astype(F32)
                fin[self.a, m] = val
            row_out[self.a, 10] = fin[self.a, 1].astype(BF16)
            self.out(10, ("x", 0), x_dev)

        def along_z(self):
            for way, sign in ((0, 1), (1, -1)):
                self.get(3 + way, ("x", 2 * sign))
                self.get(6 + way, ("r", 3 * sign))
                val = self.q(0, 2 * sign) + row_in[self.a, 3 + way].astype(F32)
                val += row_in[self.a, 6 + way].astype(F32)
                if way == self.a:
                    self.get(5, ("r", 4))
                    val += row_in[self.a, 5].astype(F32)
                row_out[self.a, 8 + way] = val.astype(BF16)
                self.out(8 + way, ("z", 2 * sign), z_at(2 * sign))

        def result(self, o, sem):
            self.get(10, ("x", 0))
            val = fin[self.a, 0] + row_in[self.a, 10].astype(F32)
            for way, sign in ((0, 1), (1, -1)):
                self.get(8 + way, ("z", 2 * sign))
                val += row_in[self.a, 8 + way].astype(F32)
            res[self.a] = val.astype(BF16)
            cp = pltpu.make_async_copy(res.at[self.a], o, sem)
            cp.start()
            outs.append(cp)

    def number(s, h):
        return lax.rem(x + s, 2) * 2 + h

    def example(ref, s, h):
        n = nz // 2
        parts = [ref[zmod(h * n + i - z + 1), s].reshape(SEQ // n, ref.shape[-1]) for i in range(n)]
        return jnp.concatenate(parts, axis=0)

    def norm_down(s, h):
        cote, he = example(cotp, s, h), example(hid, s, h)
        acc = jnp.zeros((1, width), F32)
        for j in range(nbh):
            gg = dot(he[:, j * BLK : (j + 1) * BLK], cote, 0, 0)
            acc += jnp.sum(gg * gg, axis=0, keepdims=True) * md[j : j + 1, :]
        return jnp.sum(acc)

    def norm_up(s, h):
        toke, pge = example(tokp, s, h), example(pg, s, h)
        acc = jnp.zeros((1, hidden), F32)
        for i in range(nbu):
            gg = dot(toke[:, i * BLK : (i + 1) * BLK], pge, 0, 0)
            acc += jnp.sum(gg * gg, axis=0, keepdims=True) * mu[i : i + 1, :]
        return jnp.sum(acc)

    groups = [
        [(cc_at(k, kk), cc_at(nc - k, kk)) for k, kk in near_c],
        [(xz_at(k, m), xz_at(nz - k, m)) for k, m in near_z],
    ]

    def sq_send(g):
        sq_s[g] = sq_a[...]
        for k, (dev, _) in enumerate(groups[g]):
            send(sq_s.at[g], sq_r.at[g, k], sq_ss.at[g, k], sq_rs.at[g, k], dev)

    def sq_sum(g):
        total = sq_a[...]
        for k, (_, dev) in enumerate(groups[g]):
            arrived(sq_r.at[g, k], sq_rs.at[g, k], dev)
            total += sq_r[g, k]
        sq_a[...] = total

    ro, ri = RowSum(0), RowSum(1)
    g_act[NEAR].last()
    g_act[FAR].last()
    keep(hid, hid_o, 4)
    g_pre[FAR].second()
    ro.emit(FAR, dot(half(hid, FAR), dnm[...], 1, 0))
    g_pre[NEAR].second()
    ro.emit(NEAR, dot(half(hid, NEAR), dnm[...], 1, 0))
    g_pre[FAR].last()
    ri.emit(FAR, dot(half(pg, FAR), upm[...], 1, 1))
    ro.pair_wait(FAR)
    ro.along_x((0, 1, 2, 4))
    ri.pair_wait(FAR)
    ri.along_x((0, 1, 2, 4))
    ro.pair_wait(NEAR)
    ro.along_x((3,))
    ro.next_door()
    examples = [(s, h) for s in (0, 1) for h in (0, 1)]
    down_sq = [norm_down(*e) for e in examples]
    ro.relay()

    g_pre[NEAR].last()
    keep(pg, pg_o, 5)
    ri.emit(NEAR, dot(half(pg, NEAR), upm[...], 1, 1))
    sq_a[...] = jnp.zeros_like(sq_a)
    for e, down in zip(examples, down_sq):
        sq_a[pl.ds(number(*e), 1), :] = jnp.full((1, BLK), norm_up(*e) + down)
    sq_send(0)
    ri.pair_wait(NEAR)
    ri.along_x((3,))
    ri.next_door()
    ri.relay()
    ro.near()
    ro.along_z()
    sq_sum(0)
    sq_send(1)
    ri.near()
    ri.along_z()
    ro.result(out_o, loc_sem.at[4])
    sq_sum(1)
    for p in range(nz):
        for s in (0, 1):
            e = lax.rem(x + s, 2) * 2 + lax.div(zmod(z + p - 1), nz // 2)
            bound = clip[e].astype(F32) * BOUND
            f = jnp.minimum(1.0, bound / jnp.sqrt(sq_a[pl.ds(e, 1), :] + 1e-6))
            fac[2 * p + s : 2 * p + s + 1, :] = f
    keep(fac, fac_o, 6)
    ri.result(ing_o, loc_sem.at[5])
    for cp in outs + keeps:
        cp.wait()
    for copy in pending:
        copy.wait_send()


def update(
    out_t, ing_t, tok_t, cot_t, hid_t, pg_t, mu_t, md_t, fac_t,
    out_o, ing_o, up_o, dn_o,
    out_v, ing_v, tokp, cotp, hid, pg, mu, md, fac, psc, csc, uo, do, sem, put_sem,
):
    def get(src, dst, k):
        cp = pltpu.make_async_copy(src, dst, sem.at[k])
        cp.start()
        return cp

    width, hidden = tok_t.shape[-1], hid_t.shape[-1]
    tokens = psc.shape[0]
    n = tok_t.shape[0] * tok_t.shape[1]
    run = tokens // n
    got = [
        get(fac_t, fac, 0), get(pg_t, pg, 1), get(mu_t, mu, 2), get(md_t, md, 3),
        get(tok_t, tokp, 4), get(cot_t, cotp, 5), get(hid_t, hid, 6), get(out_t, out_v, 7), get(ing_t, ing_v, 8),
    ]
    puts = []

    def put(src, dst):
        cp = pltpu.make_async_copy(src, dst, put_sem.at[len(puts)])
        cp.start()
        puts.append(cp)

    got[0].wait()
    got[1].wait()
    for i in range(n):
        rows = pg[i // 2, i % 2].astype(F32) * fac[i : i + 1, 0:1]
        psc[i * run : (i + 1) * run] = rows.astype(BF16)
    for cp in got[2:5]:
        cp.wait()
    tile = 256
    for i in range(width // tile):
        at = slice(i * tile, (i + 1) * tile)
        g2 = dot(tokp[..., at].reshape(tokens, tile), psc[...], 0, 0)
        for h in range(tile // BLK):
            lo = i * tile + h * BLK
            row = mu[lo // BLK : lo // BLK + 1, :] * UNIT
            uo[lo : lo + BLK, :] = (g2[h * BLK : (h + 1) * BLK] * row).astype(BF16)
        put(uo.at[at], up_o.at[at])
    for cp in got[5:]:
        cp.wait()
    put(out_v, out_o)
    put(ing_v, ing_o)
    for i in range(n):
        rows = cotp[i // 2, i % 2].reshape(run, width).astype(F32) * fac[i : i + 1, 0:1]
        csc[i * run : (i + 1) * run] = rows.astype(BF16)
    hf = hid[...].reshape(tokens, hidden)
    for i in range(hidden // tile):
        at = slice(i * tile, (i + 1) * tile)
        g2 = dot(hf[:, at], csc[...], 0, 0)
        for h in range(tile // BLK):
            lo = i * tile + h * BLK
            row = md[lo // BLK : lo // BLK + 1, :] * UNIT
            do[lo : lo + BLK, :] = (g2[h * BLK : (h + 1) * BLK] * row).astype(BF16)
        put(do.at[at], dn_o.at[at])
    for cp in puts:
        cp.wait()


def solution(mesh):
    nz = mesh.shape["row"] // 4
    nc = mesh.shape["col"]

    def local(tok, cot, up, dn, upk, dnk, clip):
        width, hidden = up.shape
        tokens = tok.shape[0] * mesh.shape["row"]
        blk = tokens // nc // 2
        any_, vm, sm = (pl.BlockSpec(memory_space=m) for m in (pl.ANY, pltpu.VMEM, pltpu.SMEM))
        dma = pltpu.SemaphoreType.DMA
        n_ag = 32
        n_row = 2 + len(ROW_KEYS)
        panel = jax.ShapeDtypeStruct((nz, 2, 2, SUB, width), BF16)
        rowed = jax.ShapeDtypeStruct((nz, 2, blk, hidden), BF16)
        shard = jax.ShapeDtypeStruct(tok.shape, BF16)
        up_mask = jax.ShapeDtypeStruct((16, hidden), F32)
        down_mask = jax.ShapeDtypeStruct((8, width), F32)
        factors = jax.ShapeDtypeStruct((2 * nz, BLK), F32)
        made = pl.pallas_call(
            functools.partial(kernel, nz, nc),
            out_shape=(shard, shard, panel, panel, rowed, rowed, up_mask, down_mask, factors),
            in_specs=[any_] * 4 + [sm] * 3,
            out_specs=(any_,) * 9,
            scratch_shapes=[
                pltpu.VMEM(panel.shape, BF16),
                pltpu.VMEM(panel.shape, BF16),
                pltpu.VMEM((width, hidden), BF16),
                pltpu.VMEM((hidden, width), BF16),
                pltpu.VMEM((16, hidden), F32),
                pltpu.VMEM((8, width), F32),
                pltpu.VMEM((4, nc, blk, hidden), BF16),
                pltpu.VMEM((4, nc // 2, blk // 2, hidden), BF16),
                pltpu.VMEM((4, nc // 2, blk // 2, hidden), BF16),
                pltpu.VMEM((4, blk, hidden), BF16),
                pltpu.VMEM((4, nc // 2, blk, hidden), BF16),
                pltpu.VMEM((4, blk // 2, hidden), BF16),
                pltpu.VMEM((4, nc // 2, blk // 2, hidden), BF16),
                pltpu.VMEM(rowed.shape, BF16),
                pltpu.VMEM(rowed.shape, BF16),
                pltpu.VMEM((2, blk, hidden), F32),
                pltpu.VMEM((2, nz, 2, SUB, width), F32),
                pltpu.VMEM((2, nz, 2, SUB, width), F32),
                pltpu.VMEM((2, nz, 2, SUB, width), F32),
                pltpu.VMEM((2, 11, SUB, width), BF16),
                pltpu.VMEM((2, 11, SUB, width), BF16),
                pltpu.VMEM((2, 2, 2, SUB, width), BF16),
                pltpu.VMEM((2, 2, 2, SUB, width), BF16),
                pltpu.VMEM((2, 2, SUB, width), F32),
                pltpu.VMEM((2, SUB, width), BF16),
                pltpu.VMEM((8, BLK), F32),
                pltpu.VMEM((2, 8, BLK), F32),
                pltpu.VMEM((2, 16, 8, BLK), F32),
                pltpu.VMEM((2 * nz, BLK), F32),
                dma((16,)),
                dma((2, n_ag)),
                dma((2, n_ag)),
                dma((8, 14)),
                dma((8, 14)),
                dma((2, n_row)),
                dma((2, n_row)),
                dma((2, 16)),
                dma((2, 16)),
            ],
            compiler_params=pltpu.CompilerParams(
                collective_id=0, has_side_effects=True, vmem_limit_bytes=56 * 1024 * 1024
            ),
        )(tok, cot, up, dn, upk.T, dnk, clip)
        wide = jax.ShapeDtypeStruct((tokens, width), BF16)
        grad_up = jax.ShapeDtypeStruct(up.shape, BF16)
        grad_dn = jax.ShapeDtypeStruct(dn.shape, BF16)
        held = (shard, shard, panel, panel, rowed, rowed, up_mask, down_mask, factors)
        held += (jax.ShapeDtypeStruct((tokens, hidden), BF16), wide, grad_up, grad_dn)
        return pl.pallas_call(
            update,
            out_shape=(shard, shard, grad_up, grad_dn),
            in_specs=[any_] * 9,
            out_specs=(any_,) * 4,
            scratch_shapes=[pltpu.VMEM(t.shape, t.dtype) for t in held] + [dma((16,)), dma((16,))],
            compiler_params=pltpu.CompilerParams(vmem_limit_bytes=60 * 1024 * 1024),
        )(*made)

    placed = (
        P("row", "col"),
        P("row", "col"),
        P("col", "row"),
        P("row", "col"),
        P("col", "row"),
        P("row", "col"),
        P(),
    )
    return jax.shard_map(
        local,
        mesh=mesh,
        in_specs=placed,
        out_specs=(P("row", "col"), P("row", "col"), P("col", "row"), P("row", "col")),
        check_vma=False,
    )
```

```python
import functools
import math

import jax
import jax.numpy as jnp
from jax import lax
from jax.experimental import pallas as pl
from jax.experimental.pallas import tpu as pltpu
from jax.sharding import PartitionSpec as P

MESH = pl.DeviceIdType.MESH
D = 12288
FF = 24576
SEQ = 128
BLK = 128
EX = 4
SUB = 16
F32 = jnp.float32
BF16 = jnp.bfloat16
ROOT = math.sqrt(2.0 / math.pi)
ROW_KEYS = [("x", 4), ("x", 3), ("x", -3), ("b", 2), ("b", -2), ("x", 0), ("n", 1), ("n", -1)]
ROW_KEYS += [("r", 4), ("r", 3), ("r", -3), ("z", 2), ("z", -2)]
UNIT = 7.0 / (EX * math.sqrt(SEQ))
BOUND = math.sqrt(D * FF * SEQ) / 1000.0


def dot(a, b, ca, cb):
    return lax.dot_general(a, b, (((ca,), (cb,)), ((), ())), preferred_element_type=F32)


def kernel(
    nz, nc,
    tok, cot, up, dn, upk, dnk, clip,
    out_o, ing_o, tok_o, cot_o, hid_o, pg_o, mu_o, md_o, fac_o,
    tokp, cotp, upm, dnm, mu, md,
    send_h, via_x, via_y, from_x, from_y, sum_x, sum_y, hid, pg, dact,
    part, pair, pair_r, row_out, row_in, near_out, near_in, fin, res,
    sq_a, sq_s, sq_r, fac,
    loc_sem, ag_s, ag_r, col_s, col_r, row_s, row_r, sq_ss, sq_rs,
):
    tokens = tok.shape[0] * 4 * nz
    width = tok.shape[1]
    hidden = up.shape[1]
    r = lax.axis_index("row")
    c = lax.axis_index("col")
    core = lax.rem(r, 2)
    z = lax.rem(lax.div(r, 2), nz)
    x = lax.div(r, 2 * nz)

    def row_of(xx, zz, kk):
        return (xx * nz + zz) * 2 + kk

    def zmod(v):
        return lax.rem(v + 2 * nz, nz)

    core_dev = (row_of(x, z, 1 - core), c)
    x_dev = (row_of(1 - x, z, core), c)

    def z_at(k):
        return (row_of(x, zmod(z + k), core), c)

    up_in = pltpu.make_async_copy(up, upm, loc_sem.at[0])
    dn_in = pltpu.make_async_copy(dn, dnm, loc_sem.at[1])
    up_in.start()
    dn_in.start()

    def place(off):
        return (off + 1) % nz

    own = [
        pltpu.make_async_copy(tok, tokp.at[place(0), 0, 0], loc_sem.at[2]),
        pltpu.make_async_copy(cot, cotp.at[place(0), 0, 0], loc_sem.at[3]),
    ]
    own[0].start()
    own[1].start()

    barrier = pltpu.get_barrier_semaphore()
    near_c = [(0, 1)] + [(k, kk) for k in range(1, nc) for kk in (0, 1)]
    near_z = [(0, 1)] + [(k, m) for k in range(1, nz) for m in (0, 1)]

    def cc_at(k, kk):
        return (row_of(x, z, core if kk == 0 else 1 - core), lax.rem(c + k, nc))

    def xz_at(k, m):
        return (row_of(x if m == 0 else 1 - x, zmod(z + k), core), c)

    peers = [cc_at(*p) for p in near_c] + [xz_at(*p) for p in near_z]
    for dev in peers:
        pl.semaphore_signal(barrier, inc=1, device_id=dev, device_id_type=MESH)
    pl.semaphore_wait(barrier, len(peers))
    own[0].wait()
    own[1].wait()

    pending, early = [], [0]

    def flush():
        for copy in pending[: early[0]]:
            copy.wait_send()
        del pending[: early[0]]
        early[0] = len(pending)

    def send(src, dst, ssem, rsem, dev):
        copy = pltpu.make_async_remote_copy(
            src_ref=src, dst_ref=dst, send_sem=ssem, recv_sem=rsem, device_id=dev, device_id_type=MESH
        )
        copy.start()
        pending.append(copy)
        return copy

    def arrived(dst, rsem, dev):
        pltpu.make_async_remote_copy(
            src_ref=dst, dst_ref=dst, send_sem=rsem, recv_sem=rsem, device_id=dev, device_id_type=MESH
        ).wait_recv()

    class Gather:
        def __init__(self, a, shard, panel):
            self.a, self.shard, self.panel, self.keys = a, shard, panel, {}

        def sems(self, key):
            k = self.keys.setdefault(key, len(self.keys))
            return ag_s.at[self.a, k], ag_r.at[self.a, k]

        def slot(self, stream, off, other=0):
            return self.panel.at[place(off), stream, other]

        def z_put(self, stream, off, hop, key):
            src, dst = self.slot(stream, off), self.slot(stream, off - hop)
            send(src, dst, *self.sems(key), z_at(hop))

        def take(self, stream, off, key):
            arrived(self.slot(stream, off), self.sems(key)[1], x_dev)

        def core_put(self, stream, off):
            src, dst = self.slot(stream, off), self.slot(stream, off, 1)
            send(src, dst, *self.sems(("core", stream, off % nz)), core_dev)

        def x_put(self, off):
            send(self.slot(0, off), self.slot(1, off), *self.sems(("x", off % nz)), x_dev)

        def start(self):
            for sign in (1, -1):
                self.z_put(0, 0, sign, ("z", 0, sign))
                self.z_put(0, 0, 2 * sign, ("z", 0, 2 * sign))
            self.x_put(0)
            self.core_put(0, 0)

        def partner(self):
            self.take(1, 0, ("x", 0))
            for sign in (1, -1):
                self.z_put(1, 0, sign, ("z", 1, sign))
            self.core_put(1, 0)

        def near(self):
            for sign in (-1, 1):
                self.take(0, -2 * sign, ("z", 0, 2 * sign))
                self.x_put(-2 * sign)
                self.z_put(0, -2 * sign, sign, ("z", 0, 3 * sign))
                if sign == (1, -1)[self.a]:
                    self.z_put(0, -2 * sign, 2 * sign, ("z", 0, 4))
                self.core_put(0, -2 * sign)
            for sign in (1, -1):
                self.take(0, -sign, ("z", 0, sign))
                self.core_put(0, -sign)

        def near_done(self):
            for sign in (1, -1):
                self.take(1, -sign, ("z", 1, sign))
                self.core_put(1, -sign)
            self.take(1, 2, ("x", 2))
            self.core_put(1, 2)
            self.core_wait((-1, 0, 1, 2))

        def far(self):
            for sign in (1, -1):
                self.take(0, -3 * sign, ("z", 0, 3 * sign))
                self.x_put(-3 * sign)
                self.core_put(0, -3 * sign)
            self.take(0, 4, ("z", 0, 4))
            self.x_put(4)
            self.core_put(0, 4)

        def far_done(self):
            for off in (-2, 3, -3, 4):
                self.take(1, off, ("x", off % nz))
                self.core_put(1, off)
            self.core_wait((-2, 3, -3, 4))

        def core_wait(self, offs):
            for stream in (0, 1):
                for off in offs:
                    key = ("core", stream, off % nz)
                    arrived(self.slot(stream, off, 1), self.sems(key)[1], core_dev)

    gt = Gather(0, tok, tokp)
    gc = Gather(1, cot, cotp)
    gt.start()

    nbu, nbh = width // BLK, hidden // BLK
    for i in range(nbu):
        for j in range(nbh):
            mu[i : i + 1, j * BLK : (j + 1) * BLK] = jnp.full((1, BLK), upk[j, i].astype(F32))
            md[j : j + 1, i * BLK : (i + 1) * BLK] = jnp.full((1, BLK), dnk[j, i].astype(F32))
    up_in.wait()

    @pl.loop(0, nbu)
    def _(i):
        at = pl.ds(pl.multiple_of(i * BLK, BLK), BLK)
        upm[at, :] = upm[at, :] * mu[pl.ds(i, 1), :].astype(BF16)

    dn_in.wait()

    @pl.loop(0, nbh)
    def _(j):
        at = pl.ds(pl.multiple_of(j * BLK, BLK), BLK)
        dnm[at, :] = dnm[at, :] * md[pl.ds(j, 1), :].astype(BF16)

    chunk = tokens // 2
    blk = chunk // nc
    low, high = pl.ds(0, blk // 2), pl.ds(blk // 2, blk // 2)
    ny = nc // 2
    y, xh = lax.div(c, 2), lax.rem(c, 2)
    ys = range(1, ny)
    NEAR, FAR = 0, 1

    def half(ref, ch):
        n = nz // 2
        return ref[ch * n : (ch + 1) * n].reshape(chunk, ref.shape[-1])

    def col(j, flip=0):
        return lax.rem(y + j + ny, ny) * 2 + (1 - xh if flip else xh)

    col_x = (r, col(0, 1))

    def col_y(j):
        return (r, col(j))

    class Col:
        def __init__(self, a):
            self.a, self.keys = a, {}

        def sems(self, key):
            k = self.keys.setdefault(key, len(self.keys))
            return col_s.at[self.a, k], col_r.at[self.a, k]

        def put(self, src, dst, key, dev):
            send(src, dst, *self.sems(key), dev)

        def take(self, dst, key):
            arrived(dst, self.sems(key)[1], col_x)

    class ColSum(Col):
        def first(self, value):
            a = self.a
            for b in range(nc):
                send_h[a, b] = value[b * blk : (b + 1) * blk].astype(BF16)
            for j in ys:
                self.put(send_h.at[a, col(j, 1), low], via_y.at[a, j], ("vy", j), col_y(j))
                self.put(send_h.at[a, col(j, 1), high], via_x.at[a, j], ("vx", j), col_x)
            for j in ys:
                self.put(send_h.at[a, col(j), low], from_y.at[a, j, low], ("oy", j), col_y(j))
            self.put(send_h.at[a, col(0, 1), high], from_x.at[a, high], "ox", col_x)

        def second(self):
            a = self.a
            for j in ys:
                self.take(via_x.at[a, j], ("vx", j))
                val = send_h[a, col(j), high, :].astype(F32) + via_x[a, j].astype(F32)
                sum_y[a, j] = val.astype(BF16)
                self.put(sum_y.at[a, j], from_y.at[a, j, high], ("sy", j), col_y(j))
            val = send_h[a, col(0, 1), low, :].astype(F32)
            for j in ys:
                self.take(via_y.at[a, j], ("vy", j))
                val += via_y[a, j].astype(F32)
            sum_x[a] = val.astype(BF16)
            self.put(sum_x.at[a], from_x.at[a, low], "sx", col_x)

        def total(self):
            a = self.a
            self.take(from_x.at[a, high], "ox")
            self.take(from_x.at[a, low], "sx")
            val = send_h[a, c].astype(F32) + from_x[a].astype(F32)
            for j in ys:
                self.take(from_y.at[a, j, low], ("oy", j))
                self.take(from_y.at[a, j, high], ("sy", j))
                val += from_y[a, j].astype(F32)
            return val

    class ColGather(Col):
        def __init__(self, a, panel, ch):
            Col.__init__(self, a)
            self.panel, self.ch = panel, ch

        def block(self, q, part=None):
            at = (self.ch * (nz // 2) + lax.div(q, 2), lax.rem(q, 2))
            return self.panel.at[at] if part is None else self.panel.at[at + (part,)]

        def first(self, value):
            self.panel[self.ch * (nz // 2) + lax.div(c, 2), lax.rem(c, 2)] = value.astype(BF16)
            own = self.block(c)
            self.put(own, own, "x", col_x)
            for j in ys:
                self.put(own, own, ("y", j), col_y(j))

        def second(self):
            self.take(self.block(col(0, 1)), "x")
            ref = self.block(col(0, 1), low)
            for j in ys:
                self.put(ref, ref, ("xy", j), col_y(j))
            for j in ys:
                self.take(self.block(col(-j)), ("y", j))
                ref = self.block(col(-j), high)
                self.put(ref, ref, ("yx", j), col_x)

        def last(self):
            for j in ys:
                self.take(self.block(col(-j, 1), low), ("xy", j))
                self.take(self.block(col(-j, 1), high), ("yx", j))

    s_pre, s_grad = [ColSum(0), ColSum(1)], [ColSum(2), ColSum(3)]
    g_act = [ColGather(4, hid, NEAR), ColGather(5, hid, FAR)]
    g_pre = [ColGather(6, pg, NEAR), ColGather(7, pg, FAR)]
    keeps = []

    def keep(src, dst, k):
        cp = pltpu.make_async_copy(src, dst, loc_sem.at[8 + k])
        cp.start()
        keeps.append(cp)

    def activate(ch):
        v = s_pre[ch].total()
        t = jnp.tanh(ROOT * (v + 0.044715 * (v * v * v)))
        g_act[ch].first(0.5 * v * (1.0 + t))
        dact[ch] = 0.5 * (1.0 + t) + (0.5 * ROOT) * v * (1.0 - t * t) * (1.0 + 0.134145 * (v * v))

    gt.partner()
    gc.start()
    gt.near()
    gc.partner()
    gc.near()
    gt.far()
    flush()
    gt.near_done()
    s_pre[NEAR].first(dot(half(tokp, NEAR), upm[...], 1, 0))
    gc.far()
    gt.far_done()
    s_pre[FAR].first(dot(half(tokp, FAR), upm[...], 1, 0))
    s_pre[NEAR].second()
    flush()
    gc.near_done()
    gc.far_done()
    s_grad[FAR].first(dot(half(cotp, FAR), dnm[...], 1, 1))
    s_pre[FAR].second()
    s_grad[NEAR].first(dot(half(cotp, NEAR), dnm[...], 1, 1))
    flush()
    activate(NEAR)
    s_grad[FAR].second()
    flush()
    activate(FAR)
    g_act[NEAR].second()
    s_grad[NEAR].second()
    flush()
    g_pre[FAR].first(s_grad[FAR].total() * dact[FAR])
    g_act[FAR].second()
    g_pre[NEAR].first(s_grad[NEAR].total() * dact[NEAR])
    keep(tokp, tok_o, 0)
    keep(mu, mu_o, 1)
    keep(md, md_o, 2)
    keep(cotp, cot_o, 3)

    outs = []

    class RowSum:
        def __init__(self, a):
            self.a = a

        def sems(self, k):
            return row_s.at[self.a, k], row_r.at[self.a, k]

        def emit(self, ch, value):
            n = nz // 2
            v5 = value.reshape(n, 2, 2, SUB, width)
            part[self.a, ch * n : (ch + 1) * n] = v5[:, :, 0]
            pair[self.a, ch * n : (ch + 1) * n] = v5[:, :, 1]
            at = pl.ds(ch * n, n)
            send(pair.at[self.a, at], pair_r.at[self.a, at], *self.sems(ch), core_dev)

        def pair_wait(self, ch):
            at = pl.ds(ch * (nz // 2), nz // 2)
            arrived(pair_r.at[self.a, at], self.sems(ch)[1], core_dev)

        def q(self, stream, off):
            return part[self.a, place(off), stream] + pair_r[self.a, place(off), stream]

        def key(self, name):
            return self.sems(2 + ROW_KEYS.index(name))

        def out(self, slot, name, dev):
            send(row_out.at[self.a, slot], row_in.at[self.a, slot], *self.key(name), dev)

        def get(self, slot, name):
            arrived(row_in.at[self.a, slot], self.key(name)[1], x_dev)

        def along_x(self):
            for slot, off in enumerate((4, 3, -3)):
                row_out[self.a, slot] = self.q(1, off).astype(BF16)
                self.out(slot, ("x", off), x_dev)

        def two_on(self, way):
            off = (2, -2)[way]
            row_out[self.a, 3 + way] = self.q(1, off).astype(BF16)
            self.out(3 + way, ("b", off), z_at(off))

        def next_door(self):
            for way, sign in ((0, 1), (1, -1)):
                for m in (0, 1):
                    near_out[self.a, way, m] = self.q(m, sign).astype(BF16)
                send(near_out.at[self.a, way], near_in.at[self.a, way], *self.key(("n", sign)), z_at(sign))

        def relay(self):
            sign = (1, -1)[self.a]
            for slot, off, hop in ((0, 4, 2 * sign), (1, 3, 1), (2, -3, -1)):
                self.get(slot, ("x", off))
                val = self.q(0, off) + row_in[self.a, slot].astype(F32)
                row_out[self.a, 5 + slot] = val.astype(BF16)
                self.out(5 + slot, ("r", off), z_at(hop))

        def near(self):
            for way, sign in ((0, 1), (1, -1)):
                arrived(near_in.at[self.a, way], self.key(("n", sign))[1], x_dev)
            for m in (0, 1):
                val = self.q(m, 0)
                for way in (0, 1):
                    val += near_in[self.a, way, m].astype(F32)
                if m == 1:
                    for way in (0, 1):
                        self.get(3 + way, ("b", (2, -2)[way]))
                        val += row_in[self.a, 3 + way].astype(F32)
                fin[self.a, m] = val
            row_out[self.a, 10] = fin[self.a, 1].astype(BF16)
            self.out(10, ("x", 0), x_dev)

        def along_z(self):
            for way, sign in ((0, 1), (1, -1)):
                self.get(6 + way, ("r", 3 * sign))
                val = self.q(0, 2 * sign) + row_in[self.a, 6 + way].astype(F32)
                if way == self.a:
                    self.get(5, ("r", 4))
                    val += row_in[self.a, 5].astype(F32)
                row_out[self.a, 8 + way] = val.astype(BF16)
                self.out(8 + way, ("z", 2 * sign), z_at(2 * sign))

        def result(self, o, sem):
            self.get(10, ("x", 0))
            val = fin[self.a, 0] + row_in[self.a, 10].astype(F32)
            for way, sign in ((0, 1), (1, -1)):
                self.get(8 + way, ("z", 2 * sign))
                val += row_in[self.a, 8 + way].astype(F32)
            res[self.a] = val.astype(BF16)
            cp = pltpu.make_async_copy(res.at[self.a], o, sem)
            cp.start()
            outs.append(cp)

    def number(s, h):
        return lax.rem(x + s, 2) * 2 + h

    def example(ref, s, h):
        n = nz // 2
        parts = [ref[zmod(h * n + i - z + 1), s].reshape(SEQ // n, ref.shape[-1]) for i in range(n)]
        return jnp.concatenate(parts, axis=0)

    def norm_down(s, h):
        cote, he = example(cotp, s, h), example(hid, s, h)
        acc = jnp.zeros((1, width), F32)
        for j in range(nbh):
            gg = dot(he[:, j * BLK : (j + 1) * BLK], cote, 0, 0)
            acc += jnp.sum(gg * gg, axis=0, keepdims=True) * md[j : j + 1, :]
        return jnp.sum(acc)

    def norm_up(s, h):
        toke, pge = example(tokp, s, h), example(pg, s, h)
        acc = jnp.zeros((1, hidden), F32)
        for i in range(nbu):
            gg = dot(toke[:, i * BLK : (i + 1) * BLK], pge, 0, 0)
            acc += jnp.sum(gg * gg, axis=0, keepdims=True) * mu[i : i + 1, :]
        return jnp.sum(acc)

    groups = [
        [(cc_at(k, kk), cc_at(nc - k, kk)) for k, kk in near_c],
        [(xz_at(k, m), xz_at(nz - k, m)) for k, m in near_z],
    ]

    def sq_send(g):
        sq_s[g] = sq_a[...]
        for k, (dev, _) in enumerate(groups[g]):
            send(sq_s.at[g], sq_r.at[g, k], sq_ss.at[g, k], sq_rs.at[g, k], dev)

    def sq_sum(g):
        total = sq_a[...]
        for k, (_, dev) in enumerate(groups[g]):
            arrived(sq_r.at[g, k], sq_rs.at[g, k], dev)
            total += sq_r[g, k]
        sq_a[...] = total

    ro, ri = RowSum(0), RowSum(1)
    flush()
    g_act[NEAR].last()
    g_act[FAR].last()
    keep(hid, hid_o, 4)
    ro.emit(FAR, dot(half(hid, FAR), dnm[...], 1, 0))
    g_pre[FAR].second()
    ro.emit(NEAR, dot(half(hid, NEAR), dnm[...], 1, 0))
    g_pre[NEAR].second()
    ro.pair_wait(FAR)
    ro.along_x()
    ro.two_on(1)
    flush()
    g_pre[FAR].last()
    ri.emit(FAR, dot(half(pg, FAR), upm[...], 1, 1))
    ro.pair_wait(NEAR)
    ro.two_on(0)
    ro.next_door()
    examples = [(s, h) for s in (0, 1) for h in (0, 1)]
    down_sq = [norm_down(*e) for e in examples]
    ri.pair_wait(FAR)
    ri.along_x()
    ri.two_on(1)
    ro.relay()

    flush()
    g_pre[NEAR].last()
    keep(pg, pg_o, 5)
    ri.emit(NEAR, dot(half(pg, NEAR), upm[...], 1, 1))
    sq_a[...] = jnp.zeros_like(sq_a)
    for e, down in zip(examples, down_sq):
        sq_a[pl.ds(number(*e), 1), :] = jnp.full((1, BLK), norm_up(*e) + down)
    sq_send(0)
    ri.pair_wait(NEAR)
    ri.two_on(0)
    ri.next_door()
    ri.relay()
    ro.near()
    flush()
    sq_sum(0)
    sq_send(1)
    ro.along_z()
    ri.near()
    ri.along_z()
    ro.result(out_o, loc_sem.at[4])
    flush()
    sq_sum(1)
    for p in range(nz):
        for s in (0, 1):
            e = lax.rem(x + s, 2) * 2 + lax.div(zmod(z + p - 1), nz // 2)
            bound = clip[e].astype(F32) * BOUND
            f = jnp.minimum(1.0, bound / jnp.sqrt(sq_a[pl.ds(e, 1), :] + 1e-6))
            fac[2 * p + s : 2 * p + s + 1, :] = f
    keep(fac, fac_o, 6)
    ri.result(ing_o, loc_sem.at[5])
    for cp in outs + keeps:
        cp.wait()
    for copy in pending:
        copy.wait_send()


def update(
    out_t, ing_t, tok_t, cot_t, hid_t, pg_t, mu_t, md_t, fac_t,
    out_o, ing_o, up_o, dn_o,
    out_v, ing_v, tokp, cotp, hid, pg, mu, md, fac, psc, csc, uo, do, sem, put_sem,
):
    def get(src, dst, k):
        cp = pltpu.make_async_copy(src, dst, sem.at[k])
        cp.start()
        return cp

    width, hidden = tok_t.shape[-1], hid_t.shape[-1]
    tokens = psc.shape[0]
    n = tok_t.shape[0] * tok_t.shape[1]
    run = tokens // n
    got = [
        get(fac_t, fac, 0), get(pg_t, pg, 1), get(mu_t, mu, 2), get(md_t, md, 3),
        get(tok_t, tokp, 4), get(cot_t, cotp, 5), get(hid_t, hid, 6), get(out_t, out_v, 7), get(ing_t, ing_v, 8),
    ]
    puts = []

    def put(src, dst):
        cp = pltpu.make_async_copy(src, dst, put_sem.at[len(puts)])
        cp.start()
        puts.append(cp)

    got[0].wait()
    got[1].wait()
    for i in range(n):
        rows = pg[i // 2, i % 2].astype(F32) * fac[i : i + 1, 0:1]
        psc[i * run : (i + 1) * run] = rows.astype(BF16)
    for cp in got[2:5]:
        cp.wait()
    tile = 256
    for i in range(width // tile):
        at = slice(i * tile, (i + 1) * tile)
        g2 = dot(tokp[..., at].reshape(tokens, tile), psc[...], 0, 0)
        for h in range(tile // BLK):
            lo = i * tile + h * BLK
            row = mu[lo // BLK : lo // BLK + 1, :] * UNIT
            uo[lo : lo + BLK, :] = (g2[h * BLK : (h + 1) * BLK] * row).astype(BF16)
        put(uo.at[at], up_o.at[at])
    for cp in got[5:]:
        cp.wait()
    put(out_v, out_o)
    put(ing_v, ing_o)
    for i in range(n):
        rows = cotp[i // 2, i % 2].reshape(run, width).astype(F32) * fac[i : i + 1, 0:1]
        csc[i * run : (i + 1) * run] = rows.astype(BF16)
    hf = hid[...].reshape(tokens, hidden)
    for i in range(hidden // tile):
        at = slice(i * tile, (i + 1) * tile)
        g2 = dot(hf[:, at], csc[...], 0, 0)
        for h in range(tile // BLK):
            lo = i * tile + h * BLK
            row = md[lo // BLK : lo // BLK + 1, :] * UNIT
            do[lo : lo + BLK, :] = (g2[h * BLK : (h + 1) * BLK] * row).astype(BF16)
        put(do.at[at], dn_o.at[at])
    for cp in puts:
        cp.wait()


def solution(mesh):
    nz = mesh.shape["row"] // 4
    nc = mesh.shape["col"]

    def local(tok, cot, up, dn, upk, dnk, clip):
        width, hidden = up.shape
        tokens = tok.shape[0] * mesh.shape["row"]
        blk = tokens // nc // 2
        any_, vm, sm = (pl.BlockSpec(memory_space=m) for m in (pl.ANY, pltpu.VMEM, pltpu.SMEM))
        dma = pltpu.SemaphoreType.DMA
        n_ag = 32
        n_row = 2 + len(ROW_KEYS)
        panel = jax.ShapeDtypeStruct((nz, 2, 2, SUB, width), BF16)
        rowed = jax.ShapeDtypeStruct((nz, 2, blk, hidden), BF16)
        shard = jax.ShapeDtypeStruct(tok.shape, BF16)
        up_mask = jax.ShapeDtypeStruct((16, hidden), F32)
        down_mask = jax.ShapeDtypeStruct((8, width), F32)
        factors = jax.ShapeDtypeStruct((2 * nz, BLK), F32)
        made = pl.pallas_call(
            functools.partial(kernel, nz, nc),
            out_shape=(shard, shard, panel, panel, rowed, rowed, up_mask, down_mask, factors),
            in_specs=[any_] * 4 + [sm] * 3,
            out_specs=(any_,) * 9,
            scratch_shapes=[
                pltpu.VMEM(panel.shape, BF16),
                pltpu.VMEM(panel.shape, BF16),
                pltpu.VMEM((width, hidden), BF16),
                pltpu.VMEM((hidden, width), BF16),
                pltpu.VMEM((16, hidden), F32),
                pltpu.VMEM((8, width), F32),
                pltpu.VMEM((4, nc, blk, hidden), BF16),
                pltpu.VMEM((4, nc // 2, blk // 2, hidden), BF16),
                pltpu.VMEM((4, nc // 2, blk // 2, hidden), BF16),
                pltpu.VMEM((4, blk, hidden), BF16),
                pltpu.VMEM((4, nc // 2, blk, hidden), BF16),
                pltpu.VMEM((4, blk // 2, hidden), BF16),
                pltpu.VMEM((4, nc // 2, blk // 2, hidden), BF16),
                pltpu.VMEM(rowed.shape, BF16),
                pltpu.VMEM(rowed.shape, BF16),
                pltpu.VMEM((2, blk, hidden), F32),
                pltpu.VMEM((2, nz, 2, SUB, width), F32),
                pltpu.VMEM((2, nz, 2, SUB, width), F32),
                pltpu.VMEM((2, nz, 2, SUB, width), F32),
                pltpu.VMEM((2, 11, SUB, width), BF16),
                pltpu.VMEM((2, 11, SUB, width), BF16),
                pltpu.VMEM((2, 2, 2, SUB, width), BF16),
                pltpu.VMEM((2, 2, 2, SUB, width), BF16),
                pltpu.VMEM((2, 2, SUB, width), F32),
                pltpu.VMEM((2, SUB, width), BF16),
                pltpu.VMEM((8, BLK), F32),
                pltpu.VMEM((2, 8, BLK), F32),
                pltpu.VMEM((2, 16, 8, BLK), F32),
                pltpu.VMEM((2 * nz, BLK), F32),
                dma((16,)),
                dma((2, n_ag)),
                dma((2, n_ag)),
                dma((8, 14)),
                dma((8, 14)),
                dma((2, n_row)),
                dma((2, n_row)),
                dma((2, 16)),
                dma((2, 16)),
            ],
            compiler_params=pltpu.CompilerParams(
                collective_id=0, has_side_effects=True, vmem_limit_bytes=56 * 1024 * 1024
            ),
        )(tok, cot, up, dn, upk.T, dnk, clip)
        wide = jax.ShapeDtypeStruct((tokens, width), BF16)
        grad_up = jax.ShapeDtypeStruct(up.shape, BF16)
        grad_dn = jax.ShapeDtypeStruct(dn.shape, BF16)
        held = (shard, shard, panel, panel, rowed, rowed, up_mask, down_mask, factors)
        held += (jax.ShapeDtypeStruct((tokens, hidden), BF16), wide, grad_up, grad_dn)
        return pl.pallas_call(
            update,
            out_shape=(shard, shard, grad_up, grad_dn),
            in_specs=[any_] * 9,
            out_specs=(any_,) * 4,
            scratch_shapes=[pltpu.VMEM(t.shape, t.dtype) for t in held] + [dma((16,)), dma((16,))],
            compiler_params=pltpu.CompilerParams(vmem_limit_bytes=60 * 1024 * 1024),
        )(*made)

    placed = (
        P("row", "col"),
        P("row", "col"),
        P("col", "row"),
        P("row", "col"),
        P("col", "row"),
        P("row", "col"),
        P(),
    )
    return jax.shard_map(
        local,
        mesh=mesh,
        in_specs=placed,
        out_specs=(P("row", "col"), P("row", "col"), P("col", "row"), P("row", "col")),
        check_vma=False,
    )
```
